256 devices in a mesh: slab: 64 (over x, y_lo, z), fsdp: 4 (over y_hi, core).
Axes of the slice: x: 4, y: 4 (y_hi: 2, y_lo: 2; y = y_hi * 2 + y_lo), z: 8, core: 2. Of those that a mesh axis runs over, the one named last changes fastest.
Arguments:
- fields: bfloat16 [128, 128, 128, 128], P('slab', 'fsdp'), may hold values from -6 to 6
- cotangent: bfloat16 [128, 128, 128, 128], P('slab', 'fsdp'), may hold values from -6 to 6
- spectral: bfloat16 [16, 512, 2, 128, 128], P('fsdp', 'slab'), may hold values from -3 to 3
- pointwise: bfloat16 [128, 128], replicated, may hold values from -0.5 to 0.5
- lift_bias: float32 [128], replicated, may hold values from -3 to 3
Outputs:
- field_grads: bfloat16 [128, 128, 128, 128], P('slab', 'fsdp')
- weight_grads: float32 [16, 512, 2, 128, 128], P('fsdp', 'slab')
The draws below stay inside these ranges and needn't reach their ends.
All inputs are finite; a program needn't handle non-finite values.
Results may differ from the reference program's by a relative error of at most 0.0043.
Values may be sent and summed in bfloat16 or wider, within the bound.
No kernel may reach another device: no remote copies, remote signals or barrier semaphores. Data moves between devices by JAX's collectives and lax.ppermute only.
A program may use at most 128 MiB of HBM per device.

```python
import math
import jax
import jax.numpy as jnp
from jax import lax

NX = 128
NY = 128
NZ = 128
C = 128
MX = 16
MY = 16
MZ = 16
MYZ = 512


def level_of(key, extent, pieces, low, high):
    gain, own = 1.0, jax.random.fold_in(key, 6)
    for dim, blocks in pieces:
        steps = jnp.exp(jax.random.uniform(jax.random.fold_in(own, dim), (blocks,), jnp.float32, low / len(pieces), high / len(pieces)))
        gain = gain * jnp.repeat(steps, extent[dim] // blocks).reshape([-1 if axis == dim else 1 for axis in range(len(extent))])
    return gain


def gaussian(own_key, extent, deviation, bound, split=(), held_as=jnp.bfloat16):
    result = jax.random.normal(own_key, extent, jnp.float32) * deviation
    if len(split) > 0:
        result = level_of(own_key, extent, split, -0.22, 0.18) * result
    return jnp.clip(result, min=-bound, max=bound).astype(held_as)


def setup_inputs(seed: int = 0) -> dict:
    keys = jax.random.split(jax.random.key(seed), 6)
    return {
        "fields": gaussian(keys[0], (NX, NY, NZ, C), 1.0, 6.0, ((0, 64), (1, 4))),
        "cotangent": gaussian(keys[1], (NX, NY, NZ, C), 1.0, 6.0, ((0, 64), (1, 4))),
        "spectral": gaussian(keys[2], (MX, MYZ, 2, C, C), (max(C // 32, 1)) ** -0.5, 3.0, ((0, 4), (1, 64))),
        "pointwise": gaussian(keys[3], (C, C), C ** -0.5, 0.5),
        "lift_bias": gaussian(keys[4], (C,), 0.5, 3.0, (), jnp.float32),
    }


highest = lax.Precision.HIGHEST

def phases(freqs, points, length):
    angle = 2.0 * math.pi / length * jnp.mod(freqs[:, None] * points[None, :], length).astype(jnp.float32)
    return (jnp.cos(angle), jnp.sin(angle))

def product(form, left, right):
    return jnp.einsum(form, left, right, precision=highest)

def gelu_slope(value):
    normal_cdf = 0.5 * (1.0 + lax.erf(value * (1.0 / math.sqrt(2.0))))
    return normal_cdf + value * jnp.exp(-0.5 * value * value) * (1.0 / math.sqrt(2.0 * math.pi))

def reference(fields, cotangent, spectral, pointwise, lift_bias):
    x_freq = jnp.arange(MX, dtype=jnp.int32)
    y_freq = jnp.concatenate([jnp.arange(MY, dtype=jnp.int32), NY - MY + jnp.arange(MY, dtype=jnp.int32)])
    z_freq = jnp.arange(MZ, dtype=jnp.int32)
    cos_x, sin_x = phases(x_freq, jnp.arange(NX, dtype=jnp.int32), NX)
    cos_y, sin_y = phases(y_freq, jnp.arange(NY, dtype=jnp.int32), NY)
    cos_z, sin_z = phases(z_freq, jnp.arange(NZ, dtype=jnp.int32), NZ)
    z_weight = jnp.where(z_freq == 0, 1.0, 2.0).astype(jnp.float32) / float(NX * NY * NZ)
    z_unit = jnp.ones((MZ,), jnp.float32)

    def plane_modes(plane):
        real_z = product('ync,kn->ykc', plane, cos_z)
        imag_z = -product('ync,kn->ykc', plane, sin_z)
        real_y = product('ykc,jy->jkc', real_z, cos_y) + product('ykc,jy->jkc', imag_z, sin_y)
        imag_y = product('ykc,jy->jkc', imag_z, cos_y) - product('ykc,jy->jkc', real_z, sin_y)
        return jnp.stack([real_y, imag_y], 0)

    def along_x(stacked):
        real_part = product('xjkc,mx->mjkc', stacked[:, 0], cos_x) + product('xjkc,mx->mjkc', stacked[:, 1], sin_x)
        imag_part = product('xjkc,mx->mjkc', stacked[:, 1], cos_x) - product('xjkc,mx->mjkc', stacked[:, 0], sin_x)
        return (real_part, imag_part)

    def back_x(real_part, imag_part):
        real_x = product('mjkc,mx->xjkc', real_part, cos_x) - product('mjkc,mx->xjkc', imag_part, sin_x)
        imag_x = product('mjkc,mx->xjkc', real_part, sin_x) + product('mjkc,mx->xjkc', imag_part, cos_x)
        return jnp.stack([real_x, imag_x], 1)

    def plane_cells(stacked, z_scale):
        real_y = product('jkc,jy->ykc', stacked[0], cos_y) - product('jkc,jy->ykc', stacked[1], sin_y)
        imag_y = product('jkc,jy->ykc', stacked[0], sin_y) + product('jkc,jy->ykc', stacked[1], cos_y)
        return product('ykc,kn->ync', real_y, cos_z * z_scale[:, None]) - product('ykc,kn->ync', imag_y, sin_z * z_scale[:, None])
    weights = spectral.astype(jnp.float32).reshape(MX, 2 * MY, MZ, 2, C, C)
    weight_real = weights[:, :, :, 0]
    weight_imag = weights[:, :, :, 1]
    lifted = lax.map(lambda plane: plane_modes(plane.astype(jnp.float32)), fields)
    modes_real, modes_imag = along_x(lifted)
    mixed_real = product('mjkc,mjkco->mjko', modes_real, weight_real) - product('mjkc,mjkco->mjko', modes_imag, weight_imag)
    mixed_imag = product('mjkc,mjkco->mjko', modes_real, weight_imag) + product('mjkc,mjkco->mjko', modes_imag, weight_real)

    def first_pass(items):
        plane, cot_plane, spec_plane = items
        spatial = plane_cells(spec_plane, z_weight)
        linear = jnp.dot(plane.reshape(NY * NZ, C), pointwise, preferred_element_type=jnp.float32).reshape(NY, NZ, C)
        pre = spatial + linear + lift_bias
        slope = cot_plane.astype(jnp.float32) * gelu_slope(pre)
        return (plane_modes(slope), slope.astype(jnp.bfloat16))
    grad_lifted, slope_half = lax.map(first_pass, (fields, cotangent, back_x(mixed_real, mixed_imag)))
    grad_real, grad_imag = along_x(grad_lifted)
    grad_real = grad_real * z_weight[None, None, :, None]
    grad_imag = grad_imag * z_weight[None, None, :, None]
    grad_w_real = product('mjkc,mjko->mjkco', modes_real, grad_real) + product('mjkc,mjko->mjkco', modes_imag, grad_imag)
    grad_w_imag = product('mjkc,mjko->mjkco', modes_real, grad_imag) - product('mjkc,mjko->mjkco', modes_imag, grad_real)
    weight_grads = jnp.stack([grad_w_real, grad_w_imag], 3).reshape(MX, MYZ, 2, C, C)
    back_real = product('mjko,mjkco->mjkc', grad_real, weight_real) + product('mjko,mjkco->mjkc', grad_imag, weight_imag)
    back_imag = product('mjko,mjkco->mjkc', grad_imag, weight_real) - product('mjko,mjkco->mjkc', grad_real, weight_imag)

    def second_pass(items):
        slope_plane, spec_plane = items
        spatial = plane_cells(spec_plane, z_unit)
        linear = jnp.dot(slope_plane.reshape(NY * NZ, C), pointwise.T, preferred_element_type=jnp.float32).reshape(NY, NZ, C)
        return (spatial + linear).astype(jnp.bfloat16)
    field_grads = lax.map(second_pass, (slope_half, back_x(back_real, back_imag)))
    return (field_grads, weight_grads)
```

```python
import math

import jax
import jax.numpy as jnp
import numpy as np
from jax import lax
from jax.sharding import PartitionSpec as P

MX = 16
MY = 16
MZ = 16
CORE_SWAP = [(0, 1), (1, 0), (2, 3), (3, 2)]
CHIP_SWAP = [(0, 2), (2, 0), (1, 3), (3, 1)]

highest = lax.Precision.HIGHEST


def waves(freqs, points, length):
    angle = 2.0 * math.pi / length * np.mod(np.outer(freqs, points), length)
    return np.cos(angle), np.sin(angle)


def complex_table(freqs, points, length):
    cosine, sine = waves(freqs, points, length)
    table = np.empty((len(freqs), 2, len(points), 2))
    table[:, 0, :, 0] = cosine
    table[:, 0, :, 1] = sine
    table[:, 1, :, 0] = -sine
    table[:, 1, :, 1] = cosine
    return table.astype(np.float32)


def real_table(freqs, points, length):
    cosine, sine = waves(freqs, points, length)
    return np.stack([cosine, -sine], 1).astype(np.float32)


def product(form, left, right):
    return jnp.einsum(form, left, right, precision=highest)


def gelu_slope(value):
    normal_cdf = 0.5 * (1.0 + lax.erf(value * (1.0 / math.sqrt(2.0))))
    return normal_cdf + value * jnp.exp(-0.5 * value * value) * (1.0 / math.sqrt(2.0 * math.pi))


def own_first(pair, first):
    return jnp.where(first, pair[0], pair[1]), jnp.where(first, pair[1], pair[0])


def in_order(own, other, first):
    return jnp.where(first, own, other), jnp.where(first, other, own)


def body(fields, cotangent, spectral, pointwise, lift_bias):
    x_rows, y_rows, z_cells, channels = fields.shape
    slabs = lax.axis_size("slab")
    x_total = x_rows * slabs
    y_total = y_rows * lax.axis_size("fsdp")
    scale = 1.0 / float(x_total * y_total * z_cells)
    slab = lax.axis_index("slab")
    shard = lax.axis_index("fsdp")
    core_first = shard % 2 == 0
    chip_first = shard // 2 == 0

    y_freq = np.concatenate([np.arange(MY), y_total - MY + np.arange(MY)])
    table_x = complex_table(np.arange(MX), np.arange(x_total), x_total)
    table_x = jnp.asarray(table_x.reshape(MX, 2, slabs, x_rows, 2))
    table_y = complex_table(y_freq, np.arange(y_total), y_total)
    table_y = lax.dynamic_slice_in_dim(jnp.asarray(table_y), shard * y_rows, y_rows, 2)
    table_z = jnp.asarray(real_table(np.arange(MZ), np.arange(z_cells), z_cells))
    z_freq = (slab % 2) * 8 + jnp.arange(8, dtype=jnp.int32)
    weight = jnp.where(z_freq == 0, scale, 2.0 * scale).astype(jnp.float32)

    def to_modes(field):
        lifted = product("aync,krn->aykrc", field, table_z)
        lifted = lifted.reshape(x_rows, y_rows, 2, 2, 4, 2, channels)
        planes = product("ayhgqrc,jsyr->gjhasqc", lifted, table_y)
        keep, send = own_first(planes, core_first)
        planes = keep + lax.ppermute(send, "fsdp", CORE_SWAP)
        planes = planes.astype(jnp.bfloat16).reshape(slabs, x_rows * 8, channels)
        whole = lax.all_to_all(planes, "slab", split_axis=0, concat_axis=0, tiled=True)
        whole = whole.reshape(slabs, x_rows, 2, 4, channels).astype(jnp.float32)
        modes = product("xarqc,msxar->msqc", whole, table_x)
        keep, send = own_first(modes.reshape(2, MX // 2, 2, 4, channels), chip_first)
        modes = keep + lax.ppermute(send, "fsdp", CHIP_SWAP)
        keep, send = own_first(modes.reshape(2, MX // 4, 2, 4, channels), core_first)
        other = lax.ppermute(send, "fsdp", CORE_SWAP)
        return jnp.concatenate(in_order(keep, other, core_first), 2)

    def to_cells(modes):
        keep, send = own_first((modes[:, :, :4], modes[:, :, 4:]), core_first)
        other = lax.ppermute(send, "fsdp", CORE_SWAP)
        modes = jnp.concatenate(in_order(keep, other, core_first), 0)
        other = lax.ppermute(modes, "fsdp", CHIP_SWAP)
        modes = jnp.concatenate(in_order(modes, other, chip_first), 0)
        planes = product("msqc,msxar->xarqc", modes, table_x)
        planes = planes.astype(jnp.bfloat16).reshape(slabs, x_rows * 8, channels)
        planes = lax.all_to_all(planes, "slab", split_axis=0, concat_axis=0, tiled=True)
        other = lax.ppermute(planes, "fsdp", CORE_SWAP)
        planes = jnp.stack(in_order(planes, other, core_first), 0).astype(jnp.float32)
        planes = planes.reshape(2, 2 * MY, 2, x_rows, 2, 4, channels)
        rows = product("gjhasqc,jsyr->ayhgqrc", planes, table_y)
        rows = rows.reshape(x_rows, y_rows, MZ, 2, channels)
        return product("aykrc,krn->aync", rows, table_z)

    forward_modes = to_modes(fields.astype(jnp.float32))
    weights = spectral.astype(jnp.float32)
    weight_real = weights[:, :, 0]
    weight_imag = weights[:, :, 1]

    def along(value):
        return value * weight[None, None, :, None]

    mode_real, mode_imag = forward_modes[:, 0], forward_modes[:, 1]
    mixed_real = product("mqc,mqco->mqo", mode_real, weight_real) - product(
        "mqc,mqco->mqo", mode_imag, weight_imag
    )
    mixed_imag = product("mqc,mqco->mqo", mode_real, weight_imag) + product(
        "mqc,mqco->mqo", mode_imag, weight_real
    )
    spatial = to_cells(along(jnp.stack([mixed_real, mixed_imag], 1)))
    linear = jnp.dot(
        fields.reshape(-1, channels), pointwise, preferred_element_type=jnp.float32
    ).reshape(spatial.shape)
    pre = spatial + linear + lift_bias
    slope = cotangent.astype(jnp.float32) * gelu_slope(pre)
    slope_half = slope.astype(jnp.bfloat16)
    grads = along(to_modes(slope))
    grad_real, grad_imag = grads[:, 0], grads[:, 1]
    outer_real = (
        mode_real[..., :, None] * grad_real[..., None, :]
        + mode_imag[..., :, None] * grad_imag[..., None, :]
    )
    outer_imag = (
        mode_real[..., :, None] * grad_imag[..., None, :]
        - mode_imag[..., :, None] * grad_real[..., None, :]
    )
    weight_grads = jnp.stack([outer_real, outer_imag], 2)
    back_real = product("mqo,mqco->mqc", grad_real, weight_real) + product(
        "mqo,mqco->mqc", grad_imag, weight_imag
    )
    back_imag = product("mqo,mqco->mqc", grad_imag, weight_real) - product(
        "mqo,mqco->mqc", grad_real, weight_imag
    )
    spatial_grads = to_cells(jnp.stack([back_real, back_imag], 1))
    linear_grads = jnp.dot(
        slope_half.reshape(-1, channels), pointwise.T, preferred_element_type=jnp.float32
    ).reshape(spatial_grads.shape)
    field_grads = (spatial_grads + linear_grads).astype(jnp.bfloat16)
    return (field_grads, weight_grads)


def solution(mesh):
    in_specs = (
        P("slab", "fsdp", None, None),
        P("slab", "fsdp", None, None),
        P("fsdp", "slab", None, None, None),
        P(),
        P(),
    )
    out_specs = (P("slab", "fsdp", None, None), P("fsdp", "slab", None, None, None))
    return jax.shard_map(body, mesh=mesh, in_specs=in_specs, out_specs=out_specs, check_vma=False)
```

```python
import math

import jax
import jax.numpy as jnp
import numpy as np
from jax import lax
from jax.experimental import pallas as pl
from jax.experimental.pallas import tpu as pltpu
from jax.sharding import PartitionSpec as P

MX = 16
MY = 16
MZ = 16
ROWS = 8
CORE_SWAP = [(0, 1), (1, 0), (2, 3), (3, 2)]
CHIP_SWAP = [(0, 2), (2, 0), (1, 3), (3, 1)]
VMEM_LIMIT = 40 * 1024 * 1024

f32 = jnp.float32
bf16 = jnp.bfloat16
highest = lax.Precision.HIGHEST


def waves(freqs, points, length):
    angle = 2.0 * math.pi / length * np.mod(np.outer(freqs, points), length)
    return np.cos(angle), np.sin(angle)


def complex_table(freqs, points, length):
    cosine, sine = waves(freqs, points, length)
    table = np.empty((len(freqs), 2, len(points), 2))
    table[:, 0, :, 0] = cosine
    table[:, 0, :, 1] = sine
    table[:, 1, :, 0] = -sine
    table[:, 1, :, 1] = cosine
    return table.astype(np.float32)


def real_table(freqs, points, length):
    cosine, sine = waves(freqs, points, length)
    return np.stack([cosine, -sine], 1).astype(np.float32)


def halves(table):
    table = np.asarray(table, np.float32)
    high = table.astype(bf16)
    low = (table - high.astype(np.float32)).astype(bf16)
    return jnp.asarray(high), jnp.asarray(low)


def z_waves(z_cells):
    wave = real_table(np.arange(MZ), np.arange(z_cells), z_cells).reshape(2 * MZ, z_cells)
    return jnp.asarray(wave), jnp.asarray(np.repeat(wave.T, ROWS, axis=1))


def y_waves(y_total, y_rows):
    freqs = np.concatenate([np.arange(MY), y_total - MY + np.arange(MY)])
    wave = complex_table(freqs, np.arange(y_total), y_total)
    wave = wave.reshape(2 * MY, 2, y_total // y_rows, y_rows, 2)
    wave = np.transpose(wave, (2, 0, 1, 4, 3)).reshape(y_total // y_rows, 4 * MY, 2 * y_rows)
    forward = np.tile(np.repeat(wave, 4, axis=1), (1, 1, 2))
    inverse = np.repeat(np.swapaxes(wave, 1, 2), 4, axis=2)
    return jnp.asarray(forward), jnp.asarray(inverse)


def product(form, left, right):
    return jnp.einsum(form, left, right, precision=highest)


def matmul(left, right):
    return jnp.dot(left, right, preferred_element_type=f32)


def matmul_t(left, right):
    return lax.dot_general(left, right, (((1,), (1,)), ((), ())), preferred_element_type=f32)


def split(value):
    high = value.astype(bf16)
    return high, (value - high.astype(f32)).astype(bf16)


def side(left, right):
    return jnp.concatenate([left, right], axis=1)


def parts(value):
    high = value.astype(bf16).astype(f32)
    return high, value - high


def place_of(value, mask):
    return jnp.where(mask, value, 0.0).astype(bf16)


def refine(table, value):
    high, low = split(value)
    return matmul(table, jnp.concatenate([high, high, low], axis=0))


def gelu_slope(value):
    normal_cdf = 0.5 * (1.0 + lax.erf(value * (1.0 / math.sqrt(2.0))))
    return normal_cdf + value * jnp.exp(-0.5 * value * value) * (1.0 / math.sqrt(2.0 * math.pi))


def both_planes(ref, block):
    start = block * ROWS
    shape = (ROWS * ref.shape[2], ref.shape[3])
    return side(ref[0, start:start + ROWS].reshape(shape), ref[1, start:start + ROWS].reshape(shape))


def put_planes(ref, block, value):
    start = block * ROWS
    channels = ref.shape[3]
    shape = (ROWS, ref.shape[2], channels)
    ref[0, start:start + ROWS] = value[:, :channels].reshape(shape)
    ref[1, start:start + ROWS] = value[:, channels:].reshape(shape)


def diagonal(square):
    zero = jnp.zeros_like(square)
    return jnp.concatenate([side(square, zero), side(zero, square)], axis=0)


def y_forward(core, lifted, y_table, keep, send):
    channels = keep.shape[-1]
    for half in range(2):
        for target, owner in ((keep, core), (send, 1 - core)):
            block = lifted[pl.ds(half * 16 + owner * 8, 8)]
            block = block.reshape(8 * block.shape[1], block.shape[2])
            planes = refine(y_table[...], block).reshape(2 * MY, 8, 2 * channels)
            target[:, half, 0:8, :] = planes[:, :, :channels]
            target[:, half, 8:16, :] = planes[:, :, channels:]


def y_inverse(core, own, other, yi_table, rows):
    channels = own.shape[-1]
    for half in range(2):
        for source, owner in ((own, core), (other, 1 - core)):
            planes = source[:, half].astype(f32)
            first = planes[:, 0:8, :].reshape(16 * MY, channels)
            second = planes[:, 8:16, :].reshape(16 * MY, channels)
            value = side(first, second).astype(bf16)
            result = matmul(yi_table[...], jnp.concatenate([value, value], axis=0))
            rows[pl.ds(half * 16 + owner * 8, 8)] = result.reshape(8, rows.shape[1], 2 * channels)


def z_inverse(block, rows, zi_table):
    value = rows[:, block * ROWS:(block + 1) * ROWS, :]
    return refine(zi_table[...], value.reshape(value.shape[0] * ROWS, value.shape[2]))


def put_lifted(lifted, block, value):
    lifted[:, block * ROWS:(block + 1) * ROWS, :] = value.reshape(
        lifted.shape[0], ROWS, lifted.shape[2]
    )


def lift_kernel(place, field, z_wave, y_wave, keep, send, z_table, y_table, lifted, cells, wave, sems):
    blocks = cells.shape[1] // ROWS
    copies = []
    for block in range(blocks):
        span = slice(block * ROWS, (block + 1) * ROWS)
        copies.append(pltpu.make_async_copy(field.at[:, span], cells.at[:, span], sems.at[block]))
    copies.append(pltpu.make_async_copy(y_wave.at[place[1]], wave, sems.at[blocks]))
    for copy in copies:
        copy.start()

    high, low = parts(z_wave[...])
    shape = (high.shape[0], ROWS, high.shape[1])
    row = lax.broadcasted_iota(jnp.int32, shape, 1)
    width = ROWS * high.shape[1]
    for index in range(ROWS):
        start = index * high.shape[1]
        for offset, part in ((0, high), (width, low), (2 * width, high)):
            value = place_of(part[:, None, :], row == index)
            z_table[:, offset + start:offset + start + high.shape[1]] = value.reshape(
                high.shape[0] * ROWS, high.shape[1]
            )

    for block in range(blocks):
        copies[block].wait()
        value = both_planes(cells, block)
        put_lifted(
            lifted, block, matmul(z_table[:, :2 * width], jnp.concatenate([value, value], axis=0))
        )

    copies[blocks].wait()
    high, low = parts(wave[...])
    row = lax.broadcasted_iota(jnp.int32, high.shape, 0) % 4
    lane = lax.broadcasted_iota(jnp.int32, high.shape, 1) // (high.shape[1] // 2)
    width = 2 * high.shape[1]
    for index in range(2):
        start = index * high.shape[1]
        for offset, part in ((0, high), (width, low), (2 * width, high)):
            y_table[:, offset + start:offset + start + high.shape[1]] = place_of(
                part, row == 2 * index + lane
            )
    y_forward(place[0], lifted, y_table, keep, send)


def table_kernel(place, zi_wave, yi_wave, zi_table, yi_table):
    high, low = parts(zi_wave[...])
    cells, width = high.shape
    lane = lax.broadcasted_iota(jnp.int32, high.shape, 1) % ROWS
    for index in range(ROWS):
        for offset, part in ((0, high), (width, low), (2 * width, high)):
            zi_table[index * cells:(index + 1) * cells, offset:offset + width] = place_of(
                part, lane == index
            )
    high, low = parts(yi_wave[place[1]])
    count, width = high.shape
    lane = lax.broadcasted_iota(jnp.int32, high.shape, 1) % 4
    for index in range(4):
        for offset, part in ((0, high), (width, low)):
            yi_table[index * count:(index + 1) * count, offset:offset + width] = place_of(
                part, lane == index
            )


def slope_kernel(
    place, own, other, field, cotangent, pointwise, bias, z_table, zi_table, y_table, yi_table,
    slope_half, keep, send, lifted, rows,
):
    y_inverse(place[0], own, other, yi_table, rows)
    square = diagonal(pointwise[...])
    shift = side(bias[...], bias[...])
    for block in range(rows.shape[1] // ROWS):
        spatial = z_inverse(block, rows, zi_table)
        pre = spatial + matmul(both_planes(field, block), square) + shift
        slope = both_planes(cotangent, block).astype(f32) * gelu_slope(pre)
        put_planes(slope_half, block, slope.astype(bf16))
        put_lifted(lifted, block, refine(z_table[...], slope))
    y_forward(place[0], lifted, y_table, keep, send)


def field_kernel(place, own, other, slope_half, pointwise, zi_table, yi_table, result, rows):
    y_inverse(place[0], own, other, yi_table, rows)
    square = diagonal(pointwise[...])
    for block in range(rows.shape[1] // ROWS):
        spatial = z_inverse(block, rows, zi_table)
        linear = matmul_t(both_planes(slope_half, block), square)
        put_planes(result, block, (spatial + linear).astype(bf16))


def stacked_rows(values):
    parts = [split(value) for value in values]
    rows = [part[0].astype(f32) for part in parts] + [part[1].astype(f32) for part in parts]
    return jnp.concatenate(rows, axis=0)


def only(rows, pair):
    index = lax.broadcasted_iota(jnp.int32, rows.shape, 0)
    return jnp.where(index % 8 == pair, rows, 0.0).astype(bf16)


def mix_kernel(modes, weights, mixed):
    channels = modes.shape[-1]
    rows = stacked_rows([modes[0, 0], modes[0, 1]])
    total = jnp.zeros((32, 2 * channels), f32)
    for pair in range(8):
        weight = side(weights[0, pair, 0], weights[0, pair, 1])
        total = total + matmul(only(rows, pair), weight)
    real = total[0:8] + total[16:24]
    imag = total[8:16] + total[24:32]
    mixed[0, 0] = real[:, :channels] - imag[:, channels:]
    mixed[0, 1] = real[:, channels:] + imag[:, :channels]


def adjoint_kernel(grads, weights, back):
    channels = grads.shape[-1]
    real, imag = grads[0, 0], grads[0, 1]
    rows = stacked_rows([side(real, imag), side(imag, -real)])
    total = jnp.zeros((32, channels), f32)
    for pair in range(8):
        weight = side(weights[0, pair, 0], weights[0, pair, 1])
        total = total + matmul_t(only(rows, pair), weight)
    back[0, 0] = total[0:8] + total[16:24]
    back[0, 1] = total[8:16] + total[24:32]


def outer_kernel(modes, grads, result):
    channels = modes.shape[-1]
    real, imag = grads[0, 0], grads[0, 1]
    left = stacked_rows([modes[0, 0], modes[0, 1]])
    right = stacked_rows([side(real, imag), side(imag, -real)])
    fill = channels - 48
    left = jnp.concatenate([left[:16], left[:16], left[16:], jnp.zeros((fill, channels), f32)], axis=0)
    right = jnp.concatenate([right, right[:16], jnp.zeros((fill, 2 * channels), f32)], axis=0)
    left = left.T
    right = right.astype(bf16)
    index = lax.broadcasted_iota(jnp.int32, left.shape, 1)
    for pair in range(8):
        value = matmul(jnp.where(index % 8 == pair, left, 0.0).astype(bf16), right)
        result[0, pair, 0] = value[:, :channels]
        result[0, pair, 1] = value[:, channels:]


def device_call(kernel, operands, spaces, outs, scratch, flops):
    return pl.pallas_call(
        kernel,
        in_specs=[pl.BlockSpec(memory_space=space) for space in spaces],
        out_specs=jax.tree.map(lambda _: pl.BlockSpec(memory_space=pltpu.VMEM), outs),
        out_shape=outs,
        scratch_shapes=scratch,
        compiler_params=pltpu.CompilerParams(vmem_limit_bytes=VMEM_LIMIT),
        cost_estimate=pl.CostEstimate(flops=flops, bytes_accessed=10**6, transcendentals=0),
    )(*operands)


def modes_call(kernel, operands, out):
    def spec(array):
        return pl.BlockSpec((1,) + array.shape[1:], lambda step: (step,) + (0,) * (array.ndim - 1))

    return pl.pallas_call(
        kernel,
        grid=(out.shape[0],),
        in_specs=[spec(array) for array in operands],
        out_specs=spec(out),
        out_shape=out,
        compiler_params=pltpu.CompilerParams(vmem_limit_bytes=VMEM_LIMIT),
        cost_estimate=pl.CostEstimate(flops=10**9, bytes_accessed=4 * 10**6, transcendentals=0),
    )(*operands)


def own_first(pair, first):
    return jnp.where(first, pair[0], pair[1]), jnp.where(first, pair[1], pair[0])


def in_order(own, other, first):
    return jnp.where(first, own, other), jnp.where(first, other, own)


def body(fields, cotangent, spectral, pointwise, lift_bias):
    x_rows, y_rows, z_cells, channels = fields.shape
    slabs = lax.axis_size("slab")
    x_total = x_rows * slabs
    y_total = y_rows * lax.axis_size("fsdp")
    scale = 1.0 / float(x_total * y_total * z_cells)
    slab = lax.axis_index("slab")
    shard = lax.axis_index("fsdp")
    core_first = shard % 2 == 0
    chip_first = shard // 2 == 0
    place = jnp.stack([shard % 2, shard]).astype(jnp.int32)

    table_x = complex_table(np.arange(MX), np.arange(x_total), x_total)
    table_x = jnp.asarray(table_x.reshape(MX, 2, slabs, x_rows, 2))
    z_wave, zi_wave = z_waves(z_cells)
    y_wave, yi_wave = y_waves(y_total, y_rows)
    z_freq = (slab % 2) * 8 + jnp.arange(8, dtype=jnp.int32)
    weight = jnp.where(z_freq == 0, scale, 2.0 * scale).astype(f32)

    message = jax.ShapeDtypeStruct((2 * MY, 2, 8 * x_rows, channels), f32)
    lifted = pltpu.VMEM((2 * MZ, y_rows, 2 * channels), f32)

    def along(value):
        return value * weight[None, None, :, None]

    def to_modes(keep, send):
        planes = keep + lax.ppermute(send, "fsdp", CORE_SWAP)
        planes = planes.astype(bf16).reshape(slabs, x_rows * 8, channels)
        whole_x = lax.all_to_all(planes, "slab", split_axis=0, concat_axis=0, tiled=True)
        whole_x = whole_x.reshape(slabs, x_rows, 2, 4, channels).astype(f32)
        modes = product("xarqc,msxar->msqc", whole_x, table_x)
        keep, send = own_first(modes.reshape(2, MX // 2, 2, 4, channels), chip_first)
        modes = keep + lax.ppermute(send, "fsdp", CHIP_SWAP)
        keep, send = own_first(modes.reshape(2, MX // 4, 2, 4, channels), core_first)
        other = lax.ppermute(send, "fsdp", CORE_SWAP)
        return jnp.concatenate(in_order(keep, other, core_first), 2)

    def to_planes(modes):
        keep, send = own_first((modes[:, :, :4], modes[:, :, 4:]), core_first)
        other = lax.ppermute(send, "fsdp", CORE_SWAP)
        modes = jnp.concatenate(in_order(keep, other, core_first), 0)
        other = lax.ppermute(modes, "fsdp", CHIP_SWAP)
        modes = jnp.concatenate(in_order(modes, other, chip_first), 0)
        planes = product("msqc,msxar->xarqc", modes, table_x)
        planes = planes.astype(bf16).reshape(slabs, x_rows * 8, channels)
        planes = lax.all_to_all(planes, "slab", split_axis=0, concat_axis=0, tiled=True)
        other = lax.ppermute(planes, "fsdp", CORE_SWAP)
        shape = message.shape
        return planes.reshape(shape), other.reshape(shape)

    def table(*shape):
        return jax.ShapeDtypeStruct(shape, bf16)

    smem, vmem, hbm = pltpu.SMEM, pltpu.VMEM, pltpu.HBM
    pairs = 2 * MZ * ROWS
    forms = (table(pairs, 3 * ROWS * z_cells), table(16 * MY, 24 * y_rows))
    keep, send, z_table, y_table = device_call(
        lift_kernel, (place, fields, z_wave, y_wave), (smem, hbm, vmem, hbm),
        (message, message) + forms,
        [lifted, pltpu.VMEM(fields.shape, bf16), pltpu.VMEM(y_wave.shape[1:], f32),
         pltpu.SemaphoreType.DMA((y_rows // ROWS + 1,))],
        10**9,
    )
    forms = (table(ROWS * z_cells, 3 * pairs), table(8 * y_rows, 32 * MY))
    zi_table, yi_table = device_call(
        table_kernel, (place, zi_wave, yi_wave), (smem, vmem, vmem), forms, [], 10**9
    )
    modes = to_modes(keep, send)
    mixed = along(modes_call(mix_kernel, (modes, spectral), jax.ShapeDtypeStruct(modes.shape, f32)))
    own, other = to_planes(mixed)
    bias = lift_bias.reshape(1, channels)
    slope_half, keep, send = device_call(
        slope_kernel,
        (place, own, other, fields, cotangent, pointwise, bias, z_table, zi_table, y_table, yi_table),
        (smem,) + (vmem,) * 10,
        (jax.ShapeDtypeStruct(fields.shape, bf16), message, message),
        [lifted, lifted], 4 * 10**9,
    )
    grads = along(to_modes(keep, send))
    back = modes_call(adjoint_kernel, (grads, spectral), jax.ShapeDtypeStruct(grads.shape, f32))
    weight_grads = modes_call(
        outer_kernel, (modes, grads), jax.ShapeDtypeStruct(spectral.shape, f32)
    )
    own, other = to_planes(back)
    field_grads = device_call(
        field_kernel, (place, own, other, slope_half, pointwise, zi_table, yi_table),
        (smem,) + (vmem,) * 6, jax.ShapeDtypeStruct(fields.shape, bf16), [lifted], 2 * 10**9,
    )
    return (field_grads, weight_grads)


def solution(mesh):
    in_specs = (
        P("slab", "fsdp", None, None),
        P("slab", "fsdp", None, None),
        P("fsdp", "slab", None, None, None),
        P(),
        P(),
    )
    out_specs = (P("slab", "fsdp", None, None), P("fsdp", "slab", None, None, None))
    return jax.shard_map(body, mesh=mesh, in_specs=in_specs, out_specs=out_specs, check_vma=False)
```

```python
import math

import jax
import jax.numpy as jnp
import numpy as np
from jax import lax
from jax.experimental import pallas as pl
from jax.experimental.pallas import tpu as pltpu
from jax.sharding import PartitionSpec as P

MX = 16
MY = 16
MZ = 16
ROWS = 8
CORE_SWAP = [(0, 1), (1, 0), (2, 3), (3, 2)]
CHIP_SWAP = [(0, 2), (2, 0), (1, 3), (3, 1)]
VMEM_LIMIT = 24 * 1024 * 1024

f32 = jnp.float32
bf16 = jnp.bfloat16
highest = lax.Precision.HIGHEST


def waves(freqs, points, length):
    angle = 2.0 * math.pi / length * np.mod(np.outer(freqs, points), length)
    return np.cos(angle), np.sin(angle)


def complex_table(freqs, points, length):
    cosine, sine = waves(freqs, points, length)
    table = np.empty((len(freqs), 2, len(points), 2))
    table[:, 0, :, 0] = cosine
    table[:, 0, :, 1] = sine
    table[:, 1, :, 0] = -sine
    table[:, 1, :, 1] = cosine
    return table.astype(np.float32)


def real_table(freqs, points, length):
    cosine, sine = waves(freqs, points, length)
    return np.stack([cosine, -sine], 1).astype(np.float32)


def halves(table):
    table = np.asarray(table, np.float32)
    high = table.astype(bf16)
    low = (table - high.astype(np.float32)).astype(bf16)
    return jnp.asarray(high), jnp.asarray(low)


def high_low(table):
    table = np.asarray(table, np.float32)
    high = table.astype(bf16)
    return high, (table - high.astype(np.float32)).astype(bf16)


def z_tables(z_cells):
    wave = real_table(np.arange(MZ), np.arange(z_cells), z_cells).reshape(2 * MZ, z_cells)
    wave = np.einsum("kz,uv->ukvz", wave, np.eye(2, dtype=np.float32))
    high, low = high_low(wave.reshape(4 * MZ, 2 * z_cells))
    inverse = np.concatenate([high.T, low.T, high.T, low.T], axis=1)
    return jnp.asarray(np.concatenate([high, low, inverse], axis=0))


def y_tables(y_total, y_rows):
    freqs = np.concatenate([np.arange(MY), y_total - MY + np.arange(MY)])
    wave = complex_table(freqs, np.arange(y_total), y_total)
    wave = wave.reshape(2 * MY, 2, y_total // y_rows, y_rows, 2)
    table = np.einsum("jsfyr,qp->fjsqypr", wave, np.eye(4, dtype=np.float32))
    high, low = high_low(table.reshape(y_total // y_rows, 16 * MY, 8 * y_rows))
    turned = [np.swapaxes(part, 1, 2) for part in (high, low)]
    return jnp.asarray(np.concatenate([high, low] + turned, axis=1))


def product(form, left, right):
    return jnp.einsum(form, left, right, precision=highest)


def matmul(left, right):
    return jnp.dot(left, right, preferred_element_type=f32)


def matmul_t(left, right):
    return lax.dot_general(left, right, (((1,), (1,)), ((), ())), preferred_element_type=f32)


def split(value):
    high = value.astype(bf16)
    return high, (value - high.astype(f32)).astype(bf16)


def side(left, right):
    return jnp.concatenate([left, right], axis=1)


def gelu_slope(value):
    normal_cdf = 0.5 * (1.0 + lax.erf(value * (1.0 / math.sqrt(2.0))))
    return normal_cdf + value * jnp.exp(-0.5 * value * value) * (1.0 / math.sqrt(2.0 * math.pi))


def both_planes(ref, pair):
    start = 2 * pair
    shape = (2 * ref.shape[2], ref.shape[3])
    return side(ref[0, start:start + 2].reshape(shape), ref[1, start:start + 2].reshape(shape))


def put_planes(ref, pair, value):
    start = 2 * pair
    channels = ref.shape[3]
    shape = (2, ref.shape[2], channels)
    ref[0, start:start + 2] = value[:, :channels].reshape(shape)
    ref[1, start:start + 2] = value[:, channels:].reshape(shape)


def diagonal(square):
    zero = jnp.zeros_like(square)
    return jnp.concatenate([side(square, zero), side(zero, square)], axis=0)


def folded(table, value):
    result = matmul(table, value)
    count = result.shape[0] // 2
    return result[:count] + result[count:]


def owners(core):
    for half in range(2):
        for owner in (core, 1 - core):
            yield half, pl.multiple_of(half * 16 + owner * 8, 8)


def y_forward(core, lifted, y_table, keep, send):
    channels = keep.shape[-1]
    count = 16 * MY
    for index, (half, start) in enumerate(owners(core)):
        target = send if index % 2 else keep
        block = lifted[:, pl.ds(start, 8), :]
        high, low = split(block.reshape(block.shape[0] * 8, block.shape[2]))
        planes = folded(y_table[:2 * count], high) + matmul(y_table[:count], low)
        planes = planes.reshape(2 * MY, 8, 2 * channels)
        target[:, half, 0:8, :] = planes[:, :, :channels]
        target[:, half, 8:16, :] = planes[:, :, channels:]


def y_inverse(core, own, other, y_table, rows):
    channels = own.shape[-1]
    for index, (half, start) in enumerate(owners(core)):
        planes = (other if index % 2 else own)[:, half].astype(f32)
        first = planes[:, 0:8, :].reshape(16 * MY, channels)
        second = planes[:, 8:16, :].reshape(16 * MY, channels)
        result = folded(y_table[32 * MY:], side(first, second).astype(bf16))
        rows[:, pl.ds(start, 8), :] = result.reshape(rows.shape[0], 8, 2 * channels)


def z_inverse(pair, rows, z_table):
    value = rows[2 * pair:2 * pair + 2]
    high, low = split(value.reshape(4 * MZ, value.shape[2]))
    return matmul(z_table[8 * MZ:], jnp.concatenate([high, high, low, low], axis=0))


def put_lifted(lifted, pair, value):
    lifted[2 * pair:2 * pair + 2] = value.reshape(2, 2 * MZ, value.shape[1])


def row_copies(source, target, sems):
    copies = []
    for index in range(source.shape[1] // ROWS):
        span = slice(index * ROWS, (index + 1) * ROWS)
        copies.append(
            pltpu.make_async_copy(source.at[:, span], target.at[:, span], sems.at[index])
        )
    return copies


def put_rows(cells, target, sems, index):
    span = slice(index * ROWS, (index + 1) * ROWS)
    copy = pltpu.make_async_copy(cells.at[:, span], target.at[:, span], sems.at[index])
    copy.start()
    return copy


def lift_kernel(
    place, field, z_tables, y_tables, keep, send, z_table, y_table, lifted, cells, sems, table_sems
):
    tables = [
        pltpu.make_async_copy(z_tables, z_table, table_sems.at[0]),
        pltpu.make_async_copy(y_tables.at[place[1]], y_table, table_sems.at[1]),
    ]
    copies = row_copies(field, cells, sems)
    for copy in (tables[0], *copies, tables[1]):
        copy.start()
    tables[0].wait()
    for pair in range(cells.shape[1] // 2):
        if pair % (ROWS // 2) == 0:
            copies[2 * pair // ROWS].wait()
        put_lifted(lifted, pair, folded(z_table[:8 * MZ], both_planes(cells, pair)))
    tables[1].wait()
    y_forward(place[0], lifted, y_table, keep, send)


def linear_rows(ref, pair, square, product_of):
    shape = (ROWS * ref.shape[2], ref.shape[3])
    span = slice(2 * pair, 2 * pair + ROWS)
    value = side(ref[0, span].reshape(shape), ref[1, span].reshape(shape))
    return product_of(value, square)


def slope_kernel(
    place, own, other, field, cotangent, pointwise, bias, z_table, y_table,
    slope_half, keep, send, lifted, rows, cells, sems,
):
    copies = []
    y_inverse(place[0], own, other, y_table, rows)
    square = diagonal(pointwise[...])
    shift = side(bias[...], bias[...])
    count = 2 * field.shape[2]
    for pair in range(field.shape[1] // 2):
        if pair % (ROWS // 2) == 0:
            linear = linear_rows(field, pair, square, matmul)
        start = pair % (ROWS // 2) * count
        pre = z_inverse(pair, rows, z_table) + linear[start:start + count] + shift
        slope = both_planes(cotangent, pair).astype(f32) * gelu_slope(pre)
        high, low = split(slope)
        put_planes(cells, pair, high)
        if pair % (ROWS // 2) == ROWS // 2 - 1:
            copies.append(put_rows(cells, slope_half, sems, 2 * pair // ROWS))
        put_lifted(
            lifted, pair, folded(z_table[:8 * MZ], high) + matmul(z_table[:4 * MZ], low)
        )
    y_forward(place[0], lifted, y_table, keep, send)
    for copy in copies:
        copy.wait()


def field_kernel(
    place, own, other, slope_half, pointwise, z_table, y_table, result, rows, cells, sems
):
    copies = []
    y_inverse(place[0], own, other, y_table, rows)
    square = diagonal(pointwise[...])
    count = 2 * slope_half.shape[2]
    for pair in range(rows.shape[0] // 2):
        if pair % (ROWS // 2) == 0:
            linear = linear_rows(slope_half, pair, square, matmul_t)
        start = pair % (ROWS // 2) * count
        spatial = z_inverse(pair, rows, z_table)
        put_planes(cells, pair, (spatial + linear[start:start + count]).astype(bf16))
        if pair % (ROWS // 2) == ROWS // 2 - 1:
            copies.append(put_rows(cells, result, sems, 2 * pair // ROWS))
    for copy in copies:
        copy.wait()


def stage_kernel(source, target, sems):
    copies = row_copies(source, target, sems)
    for copy in copies:
        copy.start()
    for copy in copies:
        copy.wait()


def stacked_rows(values):
    parts = [split(value) for value in values]
    rows = [part[0].astype(f32) for part in parts] + [part[1].astype(f32) for part in parts]
    return jnp.concatenate(rows, axis=0)


def only(rows, pair):
    index = lax.broadcasted_iota(jnp.int32, rows.shape, 0)
    return jnp.where(index % 8 == pair, rows, 0.0).astype(bf16)


def side_weights(own, other, pair):
    ref = other if pair // 4 else own
    block = ref.at[0, 0] if len(ref.shape) == 6 else ref.at[0]
    return side(block[pair % 4, 0], block[pair % 4, 1])


def mix_kernel(place, modes, own, other, mixed):
    channels = modes.shape[-1]
    rows = stacked_rows([modes[0, 0], modes[0, 1]])
    total = jnp.zeros((32, 2 * channels), f32)
    for pair in range(8):
        total = total + matmul(only(rows, pair), side_weights(own, other, pair))
    real = total[0:8] + total[16:24]
    imag = total[8:16] + total[24:32]
    mixed[0, 0] = real[:, :channels] - imag[:, channels:]
    mixed[0, 1] = real[:, channels:] + imag[:, :channels]


def adjoint_kernel(place, grads, own, other, back):
    channels = grads.shape[-1]
    real, imag = grads[0, 0], grads[0, 1]
    rows = stacked_rows([side(real, imag), side(imag, -real)])
    total = jnp.zeros((32, channels), f32)
    for pair in range(8):
        total = total + matmul_t(only(rows, pair), side_weights(own, other, pair))
    back[0, 0] = total[0:8] + total[16:24]
    back[0, 1] = total[8:16] + total[24:32]


def outer_kernel(place, modes, grads, result):
    channels = modes.shape[-1]
    real, imag = grads[0, 0], grads[0, 1]
    left = stacked_rows([modes[0, 0], modes[0, 1]])
    right = stacked_rows([side(real, imag), side(imag, -real)])
    fill = channels - 48
    left = jnp.concatenate([left[:16], left[:16], left[16:], jnp.zeros((fill, channels), f32)], axis=0)
    right = jnp.concatenate([right, right[:16], jnp.zeros((fill, 2 * channels), f32)], axis=0)
    left = left.T
    right = right.astype(bf16)
    index = lax.broadcasted_iota(jnp.int32, left.shape, 1)
    for pair in range(8):
        value = matmul(jnp.where(index % 8 == pair, left, 0.0).astype(bf16), right)
        result[0, pair, 0] = value[:, :channels]
        result[0, pair, 1] = value[:, channels:]


def device_call(kernel, operands, spaces, outs, out_spaces, scratch, flops):
    operands = [
        pltpu.with_memory_space_constraint(operand, space) if space is pltpu.HBM else operand
        for operand, space in zip(operands, spaces)
    ]
    return pl.pallas_call(
        kernel,
        in_specs=[pl.BlockSpec(memory_space=space) for space in spaces],
        out_specs=[pl.BlockSpec(memory_space=space) for space in out_spaces],
        out_shape=outs,
        scratch_shapes=scratch,
        compiler_params=pltpu.CompilerParams(vmem_limit_bytes=VMEM_LIMIT),
        cost_estimate=pl.CostEstimate(flops=flops, bytes_accessed=10**6, transcendentals=0),
    )(*operands)


def modes_call(kernel, place, operands, out):
    def spec(array):
        rest = (0,) * (len(array.shape) - 2)
        if len(array.shape) == 6:
            return pl.BlockSpec((1, 1) + array.shape[2:], lambda step, place: (step, place[0]) + rest)
        return pl.BlockSpec((1,) + array.shape[1:], lambda step, place: (step, 0) + rest)

    return pl.pallas_call(
        kernel,
        grid_spec=pltpu.PrefetchScalarGridSpec(
            num_scalar_prefetch=1,
            grid=(out.shape[0],),
            in_specs=[spec(array) for array in operands],
            out_specs=spec(out),
        ),
        out_shape=out,
        compiler_params=pltpu.CompilerParams(vmem_limit_bytes=VMEM_LIMIT),
        cost_estimate=pl.CostEstimate(flops=10**9, bytes_accessed=4 * 10**6, transcendentals=0),
    )(place, *operands)


def own_first(pair, first):
    return jnp.where(first, pair[0], pair[1]), jnp.where(first, pair[1], pair[0])


def in_order(own, other, first):
    return jnp.where(first, own, other), jnp.where(first, other, own)


def body(fields, cotangent, spectral, pointwise, lift_bias):
    x_rows, y_rows, z_cells, channels = fields.shape
    slabs = lax.axis_size("slab")
    x_total = x_rows * slabs
    y_total = y_rows * lax.axis_size("fsdp")
    scale = 1.0 / float(x_total * y_total * z_cells)
    slab = lax.axis_index("slab")
    shard = lax.axis_index("fsdp")
    core_first = shard % 2 == 0
    chip_first = shard // 2 == 0
    place = jnp.stack([shard % 2, shard]).astype(jnp.int32)

    table_x = complex_table(np.arange(MX), np.arange(x_total), x_total)
    table_x = jnp.asarray(table_x.reshape(MX, 2, slabs, x_rows, 2))
    z_all = z_tables(z_cells)
    y_all = y_tables(y_total, y_rows)
    z_freq = (slab % 2) * 8 + (shard % 2) * 4 + jnp.arange(8, dtype=jnp.int32) % 4
    weight = jnp.where(z_freq == 0, scale, 2.0 * scale).astype(f32)
    own_weights = spectral.reshape(MX // 4, 2, 4, 2, channels, channels)
    send = lax.dynamic_index_in_dim(own_weights, 1 - shard % 2, 1, keepdims=False)
    other_weights = lax.ppermute(send, "fsdp", CORE_SWAP)

    message = jax.ShapeDtypeStruct((2 * MY, 2, 8 * x_rows, channels), f32)
    lifted = pltpu.VMEM((y_rows, 2 * MZ, 2 * channels), f32)

    def along(value):
        return value * weight[None, None, :, None]

    def to_modes(keep, send):
        planes = keep + lax.ppermute(send, "fsdp", CORE_SWAP)
        planes = planes.astype(bf16).reshape(slabs, x_rows * 8, channels)
        whole_x = lax.all_to_all(planes, "slab", split_axis=0, concat_axis=0, tiled=True)
        whole_x = whole_x.reshape(slabs, x_rows, 2, 4, channels).astype(f32)
        modes = product("xarqc,msxar->msqc", whole_x, table_x)
        keep, send = own_first(modes.reshape(2, MX // 2, 2, 4, channels), chip_first)
        modes = keep + lax.ppermute(send, "fsdp", CHIP_SWAP)
        return jnp.concatenate(own_first(modes.reshape(2, MX // 4, 2, 4, channels), core_first), 2)

    def regroup(modes):
        other = lax.ppermute(modes[..., 4:, :], "fsdp", CORE_SWAP)
        return jnp.concatenate(in_order(modes[..., :4, :], other, core_first), -2)

    def to_planes(modes, *beside):
        modes = jnp.concatenate(in_order(modes[:, :, :4], modes[:, :, 4:], core_first), 0)
        other = lax.ppermute(modes, "fsdp", CHIP_SWAP)
        modes = jnp.concatenate(in_order(modes, other, chip_first), 0)
        planes = product("msqc,msxar->xarqc", modes, table_x)
        planes = planes.astype(bf16).reshape(slabs, x_rows * 8, channels)
        planes = lax.all_to_all(planes, "slab", split_axis=0, concat_axis=0, tiled=True)
        planes, *beside = lax.optimization_barrier((planes, *beside))
        other = lax.ppermute(planes, "fsdp", CORE_SWAP)
        shape = message.shape
        return planes.reshape(shape), other.reshape(shape), *beside

    smem, vmem, hbm = pltpu.SMEM, pltpu.VMEM, pltpu.HBM
    cells = pltpu.VMEM(fields.shape, bf16)
    sems = pltpu.SemaphoreType.DMA((y_rows // ROWS,))
    forms = (
        jax.ShapeDtypeStruct(z_all.shape, bf16), jax.ShapeDtypeStruct(y_all.shape[1:], bf16)
    )
    keep, send, z_table, y_table = device_call(
        lift_kernel, (place, fields, z_all, y_all), (smem, hbm, hbm, hbm),
        (message, message) + forms, (vmem,) * 4,
        [lifted, cells, sems, pltpu.SemaphoreType.DMA((2,))], 10**9,
    )
    modes = to_modes(keep, send)
    out = jax.ShapeDtypeStruct(modes.shape, f32)
    mixed = along(modes_call(mix_kernel, place, (modes, own_weights, other_weights), out))
    own, other = to_planes(mixed)
    bias = lift_bias.reshape(1, channels)
    slope_half, keep, send = device_call(
        slope_kernel,
        (place, own, other, fields, cotangent, pointwise, bias, z_table, y_table),
        (smem,) + (vmem,) * 8,
        (jax.ShapeDtypeStruct(fields.shape, bf16), message, message), (hbm, vmem, vmem),
        [lifted, lifted, cells, sems], 4 * 10**9,
    )
    grads = along(to_modes(keep, send))
    back = modes_call(adjoint_kernel, place, (grads, own_weights, other_weights), out)
    pair = regroup(jnp.stack([modes, grads]))
    weight_grads = modes_call(
        outer_kernel, place, (pair[0], pair[1]), jax.ShapeDtypeStruct(spectral.shape, f32)
    )
    back, slope_half = lax.optimization_barrier((back, slope_half))
    slopes, = device_call(
        stage_kernel, (slope_half,), (hbm,), (vmem(fields.shape, bf16),), (vmem,), [sems], 10**9
    )
    own, other, weight_grads, slopes = to_planes(back, weight_grads, slopes)
    field_grads, = device_call(
        field_kernel, (place, own, other, slopes, pointwise, z_table, y_table),
        (smem,) + (vmem,) * 6, (jax.ShapeDtypeStruct(fields.shape, bf16),), (hbm,),
        [lifted, cells, sems], 2 * 10**9,
    )
    return (field_grads, weight_grads)


def solution(mesh):
    in_specs = (
        P("slab", "fsdp", None, None),
        P("slab", "fsdp", None, None),
        P("fsdp", "slab", None, None, None),
        P(),
        P(),
    )
    out_specs = (P("slab", "fsdp", None, None), P("fsdp", "slab", None, None, None))
    return jax.shard_map(body, mesh=mesh, in_specs=in_specs, out_specs=out_specs, check_vma=False)
```

```python
import math

import jax
import jax.numpy as jnp
import numpy as np
from jax import lax
from jax.experimental import pallas as pl
from jax.experimental.pallas import tpu as pltpu
from jax.sharding import PartitionSpec as P

MX = 16
MY = 16
MZ = 16
ROWS = 8
CORE_SWAP = [(0, 1), (1, 0), (2, 3), (3, 2)]
CHIP_SWAP = [(0, 2), (2, 0), (1, 3), (3, 1)]
VMEM_LIMIT = 24 * 1024 * 1024

f32 = jnp.float32
bf16 = jnp.bfloat16
highest = lax.Precision.HIGHEST


def waves(freqs, points, length):
    angle = 2.0 * math.pi / length * np.mod(np.outer(freqs, points), length)
    return np.cos(angle), np.sin(angle)


def complex_table(freqs, points, length):
    cosine, sine = waves(freqs, points, length)
    table = np.empty((len(freqs), 2, len(points), 2))
    table[:, 0, :, 0] = cosine
    table[:, 0, :, 1] = sine
    table[:, 1, :, 0] = -sine
    table[:, 1, :, 1] = cosine
    return table.astype(np.float32)


def real_table(freqs, points, length):
    cosine, sine = waves(freqs, points, length)
    return np.stack([cosine, -sine], 1).astype(np.float32)


def halves(table):
    table = np.asarray(table, np.float32)
    high = table.astype(bf16)
    low = (table - high.astype(np.float32)).astype(bf16)
    return jnp.asarray(high), jnp.asarray(low)


def high_low(table):
    table = np.asarray(table, np.float32)
    high = table.astype(bf16)
    return high, (table - high.astype(np.float32)).astype(bf16)


def z_tables(z_cells):
    wave = real_table(np.arange(MZ), np.arange(z_cells), z_cells).reshape(2 * MZ, z_cells)
    wave = np.einsum("kz,uv->ukvz", wave, np.eye(2, dtype=np.float32))
    high, low = high_low(wave.reshape(4 * MZ, 2 * z_cells))
    inverse = np.concatenate([high.T, low.T, high.T, low.T], axis=1)
    return jnp.asarray(np.concatenate([high, low, inverse], axis=0))


def y_tables(y_total, y_rows):
    freqs = np.concatenate([np.arange(MY), y_total - MY + np.arange(MY)])
    wave = complex_table(freqs, np.arange(y_total), y_total)
    wave = wave.reshape(2 * MY, 2, y_total // y_rows, y_rows, 2)
    table = np.einsum("jsfyr,qp->fjsqypr", wave, np.eye(4, dtype=np.float32))
    high, low = high_low(table.reshape(y_total // y_rows, 16 * MY, 8 * y_rows))
    turned = [np.swapaxes(part, 1, 2) for part in (high, low)]
    return jnp.asarray(np.concatenate([high, low] + turned, axis=1))


def product(form, left, right):
    return jnp.einsum(form, left, right, precision=highest)


def matmul(left, right):
    return jnp.dot(left, right, preferred_element_type=f32)


def matmul_t(left, right):
    return lax.dot_general(left, right, (((1,), (1,)), ((), ())), preferred_element_type=f32)


def split(value):
    high = value.astype(bf16)
    return high, (value - high.astype(f32)).astype(bf16)


def side(left, right):
    return jnp.concatenate([left, right], axis=1)


def gelu_slope(value):
    normal_cdf = 0.5 * (1.0 + lax.erf(value * (1.0 / math.sqrt(2.0))))
    return normal_cdf + value * jnp.exp(-0.5 * value * value) * (1.0 / math.sqrt(2.0 * math.pi))


def both_planes(ref, pair):
    start = 2 * pair
    shape = (2 * ref.shape[2], ref.shape[3])
    return side(ref[0, start:start + 2].reshape(shape), ref[1, start:start + 2].reshape(shape))


def put_planes(ref, pair, value):
    start = 2 * pair
    channels = ref.shape[3]
    shape = (2, ref.shape[2], channels)
    ref[0, start:start + 2] = value[:, :channels].reshape(shape)
    ref[1, start:start + 2] = value[:, channels:].reshape(shape)


def diagonal(square):
    zero = jnp.zeros_like(square)
    return jnp.concatenate([side(square, zero), side(zero, square)], axis=0)


def folded(table, value):
    result = matmul(table, value)
    count = result.shape[0] // 2
    return result[:count] + result[count:]


def owners(core):
    for half in range(2):
        for owner in (core, 1 - core):
            yield half, pl.multiple_of(half * 16 + owner * 8, 8)


def y_forward(core, lifted, y_table, keep, send):
    channels = keep.shape[-1]
    count = 16 * MY
    for index, (half, start) in enumerate(owners(core)):
        target = send if index % 2 else keep
        block = lifted[:, pl.ds(start, 8), :]
        high, low = split(block.reshape(block.shape[0] * 8, block.shape[2]))
        planes = folded(y_table[:2 * count], high) + matmul(y_table[:count], low)
        planes = planes.reshape(2 * MY, 8, 2 * channels)
        target[:, half, 0:8, :] = planes[:, :, :channels]
        target[:, half, 8:16, :] = planes[:, :, channels:]


def y_inverse(core, own, other, y_table, rows):
    channels = own.shape[-1]
    for index, (half, start) in enumerate(owners(core)):
        planes = (other if index % 2 else own)[:, half].astype(f32)
        first = planes[:, 0:8, :].reshape(16 * MY, channels)
        second = planes[:, 8:16, :].reshape(16 * MY, channels)
        result = folded(y_table[32 * MY:], side(first, second).astype(bf16))
        rows[:, pl.ds(start, 8), :] = result.reshape(rows.shape[0], 8, 2 * channels)


def z_inverse(pair, rows, z_table):
    value = rows[2 * pair:2 * pair + 2]
    high, low = split(value.reshape(4 * MZ, value.shape[2]))
    return matmul(z_table[8 * MZ:], jnp.concatenate([high, high, low, low], axis=0))


def put_lifted(lifted, pair, value):
    lifted[2 * pair:2 * pair + 2] = value.reshape(2, 2 * MZ, value.shape[1])


def row_copies(source, target, sems):
    copies = []
    count = source.shape[1] // sems.shape[0]
    for index in range(sems.shape[0]):
        span = slice(index * count, (index + 1) * count)
        copies.append(
            pltpu.make_async_copy(source.at[:, span], target.at[:, span], sems.at[index])
        )
    return copies


def put_rows(cells, target, sems, index):
    span = slice(index * ROWS, (index + 1) * ROWS)
    copy = pltpu.make_async_copy(cells.at[:, span], target.at[:, span], sems.at[index])
    copy.start()
    return copy


def lift_kernel(
    place, field, z_tables, y_tables, keep, send, z_table, y_table, lifted, cells, sems, table_sems
):
    tables = [
        pltpu.make_async_copy(z_tables, z_table, table_sems.at[0]),
        pltpu.make_async_copy(y_tables.at[place[1]], y_table, table_sems.at[1]),
    ]
    copies = row_copies(field, cells, sems)
    for copy in (tables[0], *copies, tables[1]):
        copy.start()
    tables[0].wait()
    for pair in range(cells.shape[1] // 2):
        if pair % (ROWS // 2) == 0:
            copies[2 * pair // ROWS].wait()
        put_lifted(lifted, pair, folded(z_table[:8 * MZ], both_planes(cells, pair)))
    tables[1].wait()
    y_forward(place[0], lifted, y_table, keep, send)


def linear_rows(ref, pair, square, product_of):
    shape = (ROWS * ref.shape[2], ref.shape[3])
    span = slice(2 * pair, 2 * pair + ROWS)
    value = side(ref[0, span].reshape(shape), ref[1, span].reshape(shape))
    return product_of(value, square)


def slope_kernel(
    place, own, other, field, cotangent, pointwise, bias, z_table, y_table,
    slope_half, keep, send, lifted, rows,
):
    y_inverse(place[0], own, other, y_table, rows)
    square = diagonal(pointwise[...])
    shift = side(bias[...], bias[...])
    count = 2 * field.shape[2]
    for pair in range(field.shape[1] // 2):
        if pair % (ROWS // 2) == 0:
            linear = linear_rows(field, pair, square, matmul)
        start = pair % (ROWS // 2) * count
        pre = z_inverse(pair, rows, z_table) + linear[start:start + count] + shift
        slope = both_planes(cotangent, pair).astype(f32) * gelu_slope(pre)
        high, low = split(slope)
        put_planes(slope_half, pair, high)
        put_lifted(
            lifted, pair, folded(z_table[:8 * MZ], high) + matmul(z_table[:4 * MZ], low)
        )
    y_forward(place[0], lifted, y_table, keep, send)


def field_kernel(
    place, own, other, slope_half, pointwise, z_table, y_table, result, rows, cells, sems
):
    copies = []
    y_inverse(place[0], own, other, y_table, rows)
    square = diagonal(pointwise[...])
    count = 2 * slope_half.shape[2]
    for pair in range(rows.shape[0] // 2):
        if pair % (ROWS // 2) == 0:
            linear = linear_rows(slope_half, pair, square, matmul_t)
        start = pair % (ROWS // 2) * count
        spatial = z_inverse(pair, rows, z_table)
        put_planes(cells, pair, (spatial + linear[start:start + count]).astype(bf16))
        if pair % (ROWS // 2) == ROWS // 2 - 1:
            copies.append(put_rows(cells, result, sems, 2 * pair // ROWS))
    for copy in copies:
        copy.wait()


def stage_kernel(source, target, sems):
    copies = row_copies(source, target, sems)
    for copy in copies:
        copy.start()
    for copy in copies:
        copy.wait()


def stacked_rows(values):
    parts = [split(value) for value in values]
    rows = [part[0].astype(f32) for part in parts] + [part[1].astype(f32) for part in parts]
    return jnp.concatenate(rows, axis=0)


def only(rows, pair):
    index = lax.broadcasted_iota(jnp.int32, rows.shape, 0)
    return jnp.where(index % 8 == pair, rows, 0.0).astype(bf16)


def side_weights(core, own, other, index, pair):
    block = other.at[index] if pair // 4 else own.at[index, core]
    return side(block[pair % 4, 0], block[pair % 4, 1])


def mix_kernel(place, modes, own, other, mixed):
    channels = modes.shape[-1]
    for index in range(modes.shape[0]):
        rows = stacked_rows([modes[index, 0], modes[index, 1]])
        total = jnp.zeros((32, 2 * channels), f32)
        for pair in range(8):
            weight = side_weights(place[0], own, other, index, pair)
            total = total + matmul(only(rows, pair), weight)
        real = total[0:8] + total[16:24]
        imag = total[8:16] + total[24:32]
        mixed[index, 0] = real[:, :channels] - imag[:, channels:]
        mixed[index, 1] = real[:, channels:] + imag[:, :channels]


def adjoint_kernel(place, grads, own, other, back):
    channels = grads.shape[-1]
    for index in range(grads.shape[0]):
        real, imag = grads[index, 0], grads[index, 1]
        rows = stacked_rows([side(real, imag), side(imag, -real)])
        total = jnp.zeros((32, channels), f32)
        for pair in range(8):
            weight = side_weights(place[0], own, other, index, pair)
            total = total + matmul_t(only(rows, pair), weight)
        back[index, 0] = total[0:8] + total[16:24]
        back[index, 1] = total[8:16] + total[24:32]


def outer_kernel(modes, grads, result):
    channels = modes.shape[-1]
    real, imag = grads[0, 0], grads[0, 1]
    left = stacked_rows([modes[0, 0], modes[0, 1]])
    right = stacked_rows([side(real, imag), side(imag, -real)])
    fill = channels - 48
    left = jnp.concatenate([left[:16], left[:16], left[16:], jnp.zeros((fill, channels), f32)], axis=0)
    right = jnp.concatenate([right, right[:16], jnp.zeros((fill, 2 * channels), f32)], axis=0)
    left = left.T
    right = right.astype(bf16)
    index = lax.broadcasted_iota(jnp.int32, left.shape, 1)
    for pair in range(8):
        value = matmul(jnp.where(index % 8 == pair, left, 0.0).astype(bf16), right)
        result[0, pair, 0] = value[:, :channels]
        result[0, pair, 1] = value[:, channels:]


def device_call(kernel, operands, spaces, outs, out_spaces, scratch, flops):
    operands = [
        pltpu.with_memory_space_constraint(operand, space) if space is pltpu.HBM else operand
        for operand, space in zip(operands, spaces)
    ]
    return pl.pallas_call(
        kernel,
        in_specs=[pl.BlockSpec(memory_space=space) for space in spaces],
        out_specs=[pl.BlockSpec(memory_space=space) for space in out_spaces],
        out_shape=outs,
        scratch_shapes=scratch,
        compiler_params=pltpu.CompilerParams(vmem_limit_bytes=VMEM_LIMIT),
        cost_estimate=pl.CostEstimate(flops=flops, bytes_accessed=10**6, transcendentals=0),
    )(*operands)


def modes_call(kernel, operands, out):
    def spec(array):
        rest = (0,) * (len(array.shape) - 1)
        return pl.BlockSpec((1,) + array.shape[1:], lambda step: (step,) + rest)

    return pl.pallas_call(
        kernel,
        grid=(out.shape[0],),
        in_specs=[spec(array) for array in operands],
        out_specs=spec(out),
        out_shape=out,
        compiler_params=pltpu.CompilerParams(vmem_limit_bytes=VMEM_LIMIT),
        cost_estimate=pl.CostEstimate(flops=10**9, bytes_accessed=4 * 10**6, transcendentals=0),
    )(*operands)


def own_first(pair, first):
    return jnp.where(first, pair[0], pair[1]), jnp.where(first, pair[1], pair[0])


def in_order(own, other, first):
    return jnp.where(first, own, other), jnp.where(first, other, own)


def body(fields, cotangent, spectral, pointwise, lift_bias):
    x_rows, y_rows, z_cells, channels = fields.shape
    slabs = lax.axis_size("slab")
    x_total = x_rows * slabs
    y_total = y_rows * lax.axis_size("fsdp")
    scale = 1.0 / float(x_total * y_total * z_cells)
    slab = lax.axis_index("slab")
    shard = lax.axis_index("fsdp")
    core_first = shard % 2 == 0
    chip_first = shard // 2 == 0
    place = jnp.stack([shard % 2, shard]).astype(jnp.int32)

    table_x = complex_table(np.arange(MX), np.arange(x_total), x_total)
    table_x = jnp.asarray(table_x.reshape(MX, 2, slabs, x_rows, 2))
    z_all = z_tables(z_cells)
    y_all = y_tables(y_total, y_rows)
    z_freq = (slab % 2) * 8 + (shard % 2) * 4 + jnp.arange(8, dtype=jnp.int32) % 4
    weight = jnp.where(z_freq == 0, scale, 2.0 * scale).astype(f32)
    own_weights = spectral.reshape(MX // 4, 2, 4, 2, channels, channels)
    send = lax.dynamic_index_in_dim(own_weights, 1 - shard % 2, 1, keepdims=False)
    other_weights = lax.ppermute(send, "fsdp", CORE_SWAP)

    message = jax.ShapeDtypeStruct((2 * MY, 2, 8 * x_rows, channels), f32)
    lifted = pltpu.VMEM((y_rows, 2 * MZ, 2 * channels), f32)

    def along(value):
        return value * weight[None, None, :, None]

    def to_modes(keep, send):
        planes = keep + lax.ppermute(send, "fsdp", CORE_SWAP)
        planes = planes.astype(bf16).reshape(slabs, x_rows * 8, channels)
        whole_x = lax.all_to_all(planes, "slab", split_axis=0, concat_axis=0, tiled=True)
        whole_x = whole_x.reshape(slabs, x_rows, 2, 4, channels).astype(f32)
        modes = product("xarqc,msxar->msqc", whole_x, table_x)
        keep, send = own_first(modes.reshape(2, MX // 2, 2, 4, channels), chip_first)
        modes = keep + lax.ppermute(send, "fsdp", CHIP_SWAP)
        return jnp.concatenate(own_first(modes.reshape(2, MX // 4, 2, 4, channels), core_first), 2)

    def regroup(modes):
        other = lax.ppermute(modes[..., 4:, :], "fsdp", CORE_SWAP)
        return jnp.concatenate(in_order(modes[..., :4, :], other, core_first), -2)

    def to_planes(modes, *beside):
        modes = jnp.concatenate(in_order(modes[:, :, :4], modes[:, :, 4:], core_first), 0)
        other = lax.ppermute(modes, "fsdp", CHIP_SWAP)
        modes = jnp.concatenate(in_order(modes, other, chip_first), 0)
        planes = product("msqc,msxar->xarqc", modes, table_x)
        planes = planes.astype(bf16).reshape(slabs, x_rows * 8, channels)
        planes = lax.all_to_all(planes, "slab", split_axis=0, concat_axis=0, tiled=True)
        planes, *beside = lax.optimization_barrier((planes, *beside))
        other = lax.ppermute(planes, "fsdp", CORE_SWAP)
        shape = message.shape
        return planes.reshape(shape), other.reshape(shape), *beside

    smem, vmem, hbm = pltpu.SMEM, pltpu.VMEM, pltpu.HBM
    cells = pltpu.VMEM(fields.shape, bf16)
    sems = pltpu.SemaphoreType.DMA((y_rows // ROWS,))
    forms = (
        jax.ShapeDtypeStruct(z_all.shape, bf16), jax.ShapeDtypeStruct(y_all.shape[1:], bf16)
    )
    keep, send, z_table, y_table = device_call(
        lift_kernel, (place, fields, z_all, y_all), (smem, hbm, hbm, hbm),
        (message, message) + forms, (vmem,) * 4,
        [lifted, cells, sems, pltpu.SemaphoreType.DMA((2,))], 10**9,
    )
    modes = to_modes(keep, send)
    out = jax.ShapeDtypeStruct(modes.shape, f32)
    mixed, = device_call(
        mix_kernel, (place, modes, own_weights, other_weights), (smem,) + (vmem,) * 3,
        (out,), (vmem,), [], 10**9,
    )
    mixed = along(mixed)
    own, other = to_planes(mixed)
    bias = lift_bias.reshape(1, channels)
    slope_half, keep, send = device_call(
        slope_kernel,
        (place, own, other, fields, cotangent, pointwise, bias, z_table, y_table),
        (smem,) + (vmem,) * 8,
        (vmem(fields.shape, bf16), message, message), (vmem,) * 3,
        [lifted, lifted], 4 * 10**9,
    )
    grads = along(to_modes(keep, send))
    back, = device_call(
        adjoint_kernel, (place, grads, own_weights, other_weights), (smem,) + (vmem,) * 3,
        (out,), (vmem,), [], 10**9,
    )
    pair = regroup(jnp.stack([modes, grads]))
    weight_grads = modes_call(
        outer_kernel, (pair[0], pair[1]), jax.ShapeDtypeStruct(spectral.shape, f32)
    )
    back, slope_half = lax.optimization_barrier((back, slope_half))
    slopes, = device_call(
        stage_kernel, (slope_half,), (hbm,), (vmem(fields.shape, bf16),), (vmem,), [sems], 10**9
    )
    own, other, weight_grads, slopes = to_planes(back, weight_grads, slopes)
    field_grads, = device_call(
        field_kernel, (place, own, other, slopes, pointwise, z_table, y_table),
        (smem,) + (vmem,) * 6, (jax.ShapeDtypeStruct(fields.shape, bf16),), (hbm,),
        [lifted, cells, sems], 2 * 10**9,
    )
    return (field_grads, weight_grads)


def solution(mesh):
    in_specs = (
        P("slab", "fsdp", None, None),
        P("slab", "fsdp", None, None),
        P("fsdp", "slab", None, None, None),
        P(),
        P(),
    )
    out_specs = (P("slab", "fsdp", None, None), P("fsdp", "slab", None, None, None))
    return jax.shard_map(body, mesh=mesh, in_specs=in_specs, out_specs=out_specs, check_vma=False)
```

```python
import math

import jax
import jax.numpy as jnp
import numpy as np
from jax import lax
from jax.experimental import pallas as pl
from jax.experimental.pallas import tpu as pltpu
from jax.sharding import PartitionSpec as P

MX = 16
MY = 16
MZ = 16
ROWS = 8
CORE_SWAP = [(0, 1), (1, 0), (2, 3), (3, 2)]
CHIP_SWAP = [(0, 2), (2, 0), (1, 3), (3, 1)]
VMEM_LIMIT = 24 * 1024 * 1024

f32 = jnp.float32
bf16 = jnp.bfloat16
highest = lax.Precision.HIGHEST


def waves(freqs, points, length):
    angle = 2.0 * math.pi / length * np.mod(np.outer(freqs, points), length)
    return np.cos(angle), np.sin(angle)


def complex_table(freqs, points, length):
    cosine, sine = waves(freqs, points, length)
    table = np.empty((len(freqs), 2, len(points), 2))
    table[:, 0, :, 0] = cosine
    table[:, 0, :, 1] = sine
    table[:, 1, :, 0] = -sine
    table[:, 1, :, 1] = cosine
    return table.astype(np.float32)


def real_table(freqs, points, length):
    cosine, sine = waves(freqs, points, length)
    return np.stack([cosine, -sine], 1).astype(np.float32)


def halves(table):
    table = np.asarray(table, np.float32)
    high = table.astype(bf16)
    low = (table - high.astype(np.float32)).astype(bf16)
    return jnp.asarray(high), jnp.asarray(low)


def high_low(table):
    table = np.asarray(table, np.float32)
    high = table.astype(bf16)
    return high, (table - high.astype(np.float32)).astype(bf16)


def z_tables(z_cells):
    wave = real_table(np.arange(MZ), np.arange(z_cells), z_cells).reshape(2 * MZ, z_cells)
    wave = np.einsum("kz,uv->ukvz", wave, np.eye(2, dtype=np.float32))
    high, low = high_low(wave.reshape(4 * MZ, 2 * z_cells))
    inverse = np.concatenate([high.T, low.T, high.T, low.T], axis=1)
    return jnp.asarray(np.concatenate([high, low, inverse], axis=0))


def y_tables(y_total, y_rows):
    freqs = np.concatenate([np.arange(MY), y_total - MY + np.arange(MY)])
    wave = complex_table(freqs, np.arange(y_total), y_total)
    wave = wave.reshape(2 * MY, 2, y_total // y_rows, y_rows, 2)
    table = np.einsum("jsfyr,qp->fjsqypr", wave, np.eye(4, dtype=np.float32))
    high, low = high_low(table.reshape(y_total // y_rows, 16 * MY, 8 * y_rows))
    turned = [np.swapaxes(part, 1, 2) for part in (high, low)]
    return jnp.asarray(np.concatenate([high, low] + turned, axis=1))


def product(form, left, right):
    return jnp.einsum(form, left, right, precision=highest)


def matmul(left, right):
    return jnp.dot(left, right, preferred_element_type=f32)


def matmul_t(left, right):
    return lax.dot_general(left, right, (((1,), (1,)), ((), ())), preferred_element_type=f32)


def split(value):
    high = value.astype(bf16)
    return high, (value - high.astype(f32)).astype(bf16)


def side(left, right):
    return jnp.concatenate([left, right], axis=1)


def gelu_slope(value):
    normal_cdf = 0.5 * (1.0 + lax.erf(value * (1.0 / math.sqrt(2.0))))
    return normal_cdf + value * jnp.exp(-0.5 * value * value) * (1.0 / math.sqrt(2.0 * math.pi))


def both_planes(ref, pair):
    start = 2 * pair
    shape = (2 * ref.shape[2], ref.shape[3])
    return side(ref[0, start:start + 2].reshape(shape), ref[1, start:start + 2].reshape(shape))


def put_planes(ref, pair, value):
    start = 2 * pair
    channels = ref.shape[3]
    shape = (2, ref.shape[2], channels)
    ref[0, start:start + 2] = value[:, :channels].reshape(shape)
    ref[1, start:start + 2] = value[:, channels:].reshape(shape)


def diagonal(square):
    zero = jnp.zeros_like(square)
    return jnp.concatenate([side(square, zero), side(zero, square)], axis=0)


def folded(table, value):
    result = matmul(table, value)
    count = result.shape[0] // 2
    return result[:count] + result[count:]


def first_row(half, owner):
    return pl.multiple_of(half * 16 + owner * 8, 8)


def y_forward(owner, lifted, y_table, target):
    channels = target.shape[-1]
    count = 16 * MY
    for half in range(2):
        block = lifted[:, pl.ds(first_row(half, owner), 8), :]
        high, low = split(block.reshape(block.shape[0] * 8, block.shape[2]))
        planes = folded(y_table[:2 * count], high) + matmul(y_table[:count], low)
        planes = planes.reshape(2 * MY, 8, 2 * channels)
        target[:, half, 0:8, :] = planes[:, :, :channels]
        target[:, half, 8:16, :] = planes[:, :, channels:]


def y_inverse(source, half, y_table):
    channels = source.shape[-1]
    planes = source[:, half].astype(f32)
    first = planes[:, 0:8, :].reshape(16 * MY, channels)
    second = planes[:, 8:16, :].reshape(16 * MY, channels)
    result = folded(y_table[32 * MY:], side(first, second).astype(bf16))
    return result.reshape(result.shape[0] // 8, 8, 2 * channels)


def keep_kernel(place, lifted, y_table, keep):
    y_forward(place[0], lifted, y_table, keep)


def keep_slopes_kernel(place, lifted, y_table, slopes, keep, slope_half, sems):
    copies = row_copies(slopes, slope_half, sems)
    for copy in copies:
        copy.start()
    y_forward(place[0], lifted, y_table, keep)
    for copy in copies:
        copy.wait()


def own_kernel(own, y_table, own_rows):
    for half in range(2):
        own_rows[half] = y_inverse(own, half, y_table)


def join_rows(core, own_rows, other, y_table, rows):
    for half in range(2):
        rows[:, pl.ds(first_row(half, core), 8), :] = own_rows[half]
        rows[:, pl.ds(first_row(half, 1 - core), 8), :] = y_inverse(other, half, y_table)


def z_inverse(pair, rows, z_table):
    value = rows[2 * pair:2 * pair + 2]
    high, low = split(value.reshape(4 * MZ, value.shape[2]))
    return matmul(z_table[8 * MZ:], jnp.concatenate([high, high, low, low], axis=0))


def put_lifted(lifted, pair, value):
    lifted[2 * pair:2 * pair + 2] = value.reshape(2, 2 * MZ, value.shape[1])


def row_copies(source, target, sems):
    copies = []
    count = source.shape[1] // sems.shape[0]
    for index in range(sems.shape[0]):
        span = slice(index * count, (index + 1) * count)
        copies.append(
            pltpu.make_async_copy(source.at[:, span], target.at[:, span], sems.at[index])
        )
    return copies


def put_rows(cells, target, sems, index):
    span = slice(index * ROWS, (index + 1) * ROWS)
    copy = pltpu.make_async_copy(cells.at[:, span], target.at[:, span], sems.at[index])
    copy.start()
    return copy


def lift_kernel(
    place, field, z_tables, y_tables, send, lifted, z_table, y_table, cells, sems, table_sems
):
    tables = [
        pltpu.make_async_copy(z_tables, z_table, table_sems.at[0]),
        pltpu.make_async_copy(y_tables.at[place[1]], y_table, table_sems.at[1]),
    ]
    copies = row_copies(field, cells, sems)
    for copy in (tables[0], *copies, tables[1]):
        copy.start()
    tables[0].wait()
    for pair in range(cells.shape[1] // 2):
        if pair % (ROWS // 2) == 0:
            copies[2 * pair // ROWS].wait()
        put_lifted(lifted, pair, folded(z_table[:8 * MZ], both_planes(cells, pair)))
    tables[1].wait()
    y_forward(1 - place[0], lifted, y_table, send)


def linear_rows(ref, pair, square, product_of):
    shape = (ROWS * ref.shape[2], ref.shape[3])
    span = slice(2 * pair, 2 * pair + ROWS)
    value = side(ref[0, span].reshape(shape), ref[1, span].reshape(shape))
    return product_of(value, square)


def slope_kernel(
    place, own_rows, other, field, cotangent, pointwise, bias, z_table, y_table,
    slope_half, send, lifted, rows,
):
    join_rows(place[0], own_rows, other, y_table, rows)
    square = diagonal(pointwise[...])
    shift = side(bias[...], bias[...])
    count = 2 * field.shape[2]
    for pair in range(field.shape[1] // 2):
        if pair % (ROWS // 2) == 0:
            linear = linear_rows(field, pair, square, matmul)
        start = pair % (ROWS // 2) * count
        pre = z_inverse(pair, rows, z_table) + linear[start:start + count] + shift
        slope = both_planes(cotangent, pair).astype(f32) * gelu_slope(pre)
        high, low = split(slope)
        put_planes(slope_half, pair, high)
        put_lifted(
            lifted, pair, folded(z_table[:8 * MZ], high) + matmul(z_table[:4 * MZ], low)
        )
    y_forward(1 - place[0], lifted, y_table, send)


def field_kernel(
    place, own_rows, other, slope_half, pointwise, z_table, y_table, result, rows, cells, sems
):
    copies = []
    join_rows(place[0], own_rows, other, y_table, rows)
    square = diagonal(pointwise[...])
    count = 2 * slope_half.shape[2]
    for pair in range(rows.shape[0] // 2):
        if pair % (ROWS // 2) == 0:
            linear = linear_rows(slope_half, pair, square, matmul_t)
        start = pair % (ROWS // 2) * count
        spatial = z_inverse(pair, rows, z_table)
        put_planes(cells, pair, (spatial + linear[start:start + count]).astype(bf16))
        if pair % (ROWS // 2) == ROWS // 2 - 1:
            copies.append(put_rows(cells, result, sems, 2 * pair // ROWS))
    for copy in copies:
        copy.wait()


def stage_kernel(source, target, sems):
    copies = row_copies(source, target, sems)
    for copy in copies:
        copy.start()
    for copy in copies:
        copy.wait()


def stacked_rows(values):
    parts = [split(value) for value in values]
    rows = [part[0].astype(f32) for part in parts] + [part[1].astype(f32) for part in parts]
    return jnp.concatenate(rows, axis=0)


def only(rows, pair):
    index = lax.broadcasted_iota(jnp.int32, rows.shape, 0)
    return jnp.where(index % 8 == pair, rows, 0.0).astype(bf16)


def side_weights(core, own, other, index, pair):
    block = other.at[index] if pair // 4 else own.at[index, core]
    return side(block[pair % 4, 0], block[pair % 4, 1])


def mix_kernel(place, modes, own, other, mixed):
    channels = modes.shape[-1]
    for index in range(modes.shape[0]):
        rows = stacked_rows([modes[index, 0], modes[index, 1]])
        total = jnp.zeros((32, 2 * channels), f32)
        for pair in range(8):
            weight = side_weights(place[0], own, other, index, pair)
            total = total + matmul(only(rows, pair), weight)
        real = total[0:8] + total[16:24]
        imag = total[8:16] + total[24:32]
        mixed[index, 0] = real[:, :channels] - imag[:, channels:]
        mixed[index, 1] = real[:, channels:] + imag[:, :channels]


def adjoint_kernel(place, grads, own, other, back):
    channels = grads.shape[-1]
    for index in range(grads.shape[0]):
        real, imag = grads[index, 0], grads[index, 1]
        rows = stacked_rows([side(real, imag), side(imag, -real)])
        total = jnp.zeros((32, channels), f32)
        for pair in range(8):
            weight = side_weights(place[0], own, other, index, pair)
            total = total + matmul_t(only(rows, pair), weight)
        back[index, 0] = total[0:8] + total[16:24]
        back[index, 1] = total[8:16] + total[24:32]


def outer_kernel(modes, grads, result):
    channels = modes.shape[-1]
    real, imag = grads[0, 0], grads[0, 1]
    left = stacked_rows([modes[0, 0], modes[0, 1]])
    right = stacked_rows([side(real, imag), side(imag, -real)])
    fill = channels - 48
    left = jnp.concatenate([left[:16], left[:16], left[16:], jnp.zeros((fill, channels), f32)], axis=0)
    right = jnp.concatenate([right, right[:16], jnp.zeros((fill, 2 * channels), f32)], axis=0)
    left = left.T
    right = right.astype(bf16)
    index = lax.broadcasted_iota(jnp.int32, left.shape, 1)
    for pair in range(8):
        value = matmul(jnp.where(index % 8 == pair, left, 0.0).astype(bf16), right)
        result[0, pair, 0] = value[:, :channels]
        result[0, pair, 1] = value[:, channels:]


def device_call(kernel, operands, spaces, outs, out_spaces, scratch, flops):
    operands = [
        pltpu.with_memory_space_constraint(operand, space) if space is pltpu.HBM else operand
        for operand, space in zip(operands, spaces)
    ]
    return pl.pallas_call(
        kernel,
        in_specs=[pl.BlockSpec(memory_space=space) for space in spaces],
        out_specs=[pl.BlockSpec(memory_space=space) for space in out_spaces],
        out_shape=outs,
        scratch_shapes=scratch,
        compiler_params=pltpu.CompilerParams(vmem_limit_bytes=VMEM_LIMIT),
        cost_estimate=pl.CostEstimate(flops=flops, bytes_accessed=10**6, transcendentals=0),
    )(*operands)


def modes_call(kernel, operands, out):
    def spec(array):
        rest = (0,) * (len(array.shape) - 1)
        return pl.BlockSpec((1,) + array.shape[1:], lambda step: (step,) + rest)

    return pl.pallas_call(
        kernel,
        grid=(out.shape[0],),
        in_specs=[spec(array) for array in operands],
        out_specs=spec(out),
        out_shape=out,
        compiler_params=pltpu.CompilerParams(vmem_limit_bytes=VMEM_LIMIT),
        cost_estimate=pl.CostEstimate(flops=10**9, bytes_accessed=4 * 10**6, transcendentals=0),
    )(*operands)


def own_first(pair, first):
    return jnp.where(first, pair[0], pair[1]), jnp.where(first, pair[1], pair[0])


def in_order(own, other, first):
    return jnp.where(first, own, other), jnp.where(first, other, own)


def body(fields, cotangent, spectral, pointwise, lift_bias):
    x_rows, y_rows, z_cells, channels = fields.shape
    slabs = lax.axis_size("slab")
    x_total = x_rows * slabs
    y_total = y_rows * lax.axis_size("fsdp")
    scale = 1.0 / float(x_total * y_total * z_cells)
    slab = lax.axis_index("slab")
    shard = lax.axis_index("fsdp")
    core_first = shard % 2 == 0
    chip_first = shard // 2 == 0
    place = jnp.stack([shard % 2, shard]).astype(jnp.int32)

    table_x = complex_table(np.arange(MX), np.arange(x_total), x_total)
    table_x = jnp.asarray(table_x.reshape(MX, 2, slabs, x_rows, 2))
    z_all = z_tables(z_cells)
    y_all = y_tables(y_total, y_rows)
    z_freq = (slab % 2) * 8 + (shard % 2) * 4 + jnp.arange(8, dtype=jnp.int32) % 4
    weight = jnp.where(z_freq == 0, scale, 2.0 * scale).astype(f32)
    own_weights = spectral.reshape(MX // 4, 2, 4, 2, channels, channels)
    send = lax.dynamic_index_in_dim(own_weights, 1 - shard % 2, 1, keepdims=False)
    other_weights = lax.ppermute(send, "fsdp", CORE_SWAP)

    message = jax.ShapeDtypeStruct((2 * MY, 2, 8 * x_rows, channels), f32)
    lifted_form = pltpu.VMEM((y_rows, 2 * MZ, 2 * channels), f32)
    own_form = pltpu.VMEM((2, y_rows, 8, 2 * channels), f32)

    def along(value):
        return value * weight[None, None, :, None]

    def to_modes(send, keep):
        planes = keep + lax.ppermute(send, "fsdp", CORE_SWAP)
        planes = planes.astype(bf16).reshape(slabs, x_rows * 8, channels)
        whole_x = lax.all_to_all(planes, "slab", split_axis=0, concat_axis=0, tiled=True)
        whole_x = whole_x.reshape(slabs, x_rows, 2, 4, channels).astype(f32)
        modes = product("xarqc,msxar->msqc", whole_x, table_x)
        keep, send = own_first(modes.reshape(2, MX // 2, 2, 4, channels), chip_first)
        modes = keep + lax.ppermute(send, "fsdp", CHIP_SWAP)
        return jnp.concatenate(own_first(modes.reshape(2, MX // 4, 2, 4, channels), core_first), 2)

    def regroup(modes):
        other = lax.ppermute(modes[..., 4:, :], "fsdp", CORE_SWAP)
        return jnp.concatenate(in_order(modes[..., :4, :], other, core_first), -2)

    def to_planes(modes, *beside):
        modes = jnp.concatenate(in_order(modes[:, :, :4], modes[:, :, 4:], core_first), 0)
        other = lax.ppermute(modes, "fsdp", CHIP_SWAP)
        modes = jnp.concatenate(in_order(modes, other, chip_first), 0)
        planes = product("msqc,msxar->xarqc", modes, table_x)
        planes = planes.astype(bf16).reshape(slabs, x_rows * 8, channels)
        planes = lax.all_to_all(planes, "slab", split_axis=0, concat_axis=0, tiled=True)
        planes, *beside = lax.optimization_barrier((planes, *beside))
        other = lax.ppermute(planes, "fsdp", CORE_SWAP)
        planes = planes.reshape(message.shape)
        own_rows, = device_call(
            own_kernel, (planes, y_table), (vmem, vmem), (own_form,), (vmem,), [], 10**9
        )
        return own_rows, other.reshape(message.shape), *beside

    smem, vmem, hbm = pltpu.SMEM, pltpu.VMEM, pltpu.HBM
    cells = pltpu.VMEM(fields.shape, bf16)
    sems = pltpu.SemaphoreType.DMA((y_rows // ROWS,))
    forms = (
        jax.ShapeDtypeStruct(z_all.shape, bf16), jax.ShapeDtypeStruct(y_all.shape[1:], bf16)
    )
    send, lifted, z_table, y_table = device_call(
        lift_kernel, (place, fields, z_all, y_all), (smem, hbm, hbm, hbm),
        (message, lifted_form) + forms, (vmem,) * 4,
        [cells, sems, pltpu.SemaphoreType.DMA((2,))], 10**9,
    )
    keep, = device_call(
        keep_kernel, (place, lifted, y_table), (smem, vmem, vmem), (message,), (vmem,), [], 10**9
    )
    modes = to_modes(send, keep)
    out = jax.ShapeDtypeStruct(modes.shape, f32)
    mixed, = device_call(
        mix_kernel, (place, modes, own_weights, other_weights), (smem,) + (vmem,) * 3,
        (out,), (vmem,), [], 10**9,
    )
    mixed = along(mixed)
    own_rows, other = to_planes(mixed)
    bias = lift_bias.reshape(1, channels)
    slopes, send, lifted = device_call(
        slope_kernel,
        (place, own_rows, other, fields, cotangent, pointwise, bias, z_table, y_table),
        (smem,) + (vmem,) * 8,
        (vmem(fields.shape, bf16), message, lifted_form), (vmem,) * 3,
        [lifted_form], 4 * 10**9,
    )
    keep, slope_half = device_call(
        keep_slopes_kernel, (place, lifted, y_table, slopes), (smem, vmem, vmem, vmem),
        (message, jax.ShapeDtypeStruct(fields.shape, bf16)), (vmem, hbm), [sems], 10**9,
    )
    grads = along(to_modes(send, keep))
    back, = device_call(
        adjoint_kernel, (place, grads, own_weights, other_weights), (smem,) + (vmem,) * 3,
        (out,), (vmem,), [], 10**9,
    )
    pair = regroup(jnp.stack([modes, grads]))
    weight_grads = modes_call(
        outer_kernel, (pair[0], pair[1]), jax.ShapeDtypeStruct(spectral.shape, f32)
    )
    back, slope_half = lax.optimization_barrier((back, slope_half))
    slopes, = device_call(
        stage_kernel, (slope_half,), (hbm,), (vmem(fields.shape, bf16),), (vmem,), [sems], 10**9
    )
    own_rows, other, weight_grads, slopes = to_planes(back, weight_grads, slopes)
    field_grads, = device_call(
        field_kernel, (place, own_rows, other, slopes, pointwise, z_table, y_table),
        (smem,) + (vmem,) * 6, (jax.ShapeDtypeStruct(fields.shape, bf16),), (hbm,),
        [lifted_form, cells, sems], 2 * 10**9,
    )
    return (field_grads, weight_grads)


def solution(mesh):
    in_specs = (
        P("slab", "fsdp", None, None),
        P("slab", "fsdp", None, None),
        P("fsdp", "slab", None, None, None),
        P(),
        P(),
    )
    out_specs = (P("slab", "fsdp", None, None), P("fsdp", "slab", None, None, None))
    return jax.shard_map(body, mesh=mesh, in_specs=in_specs, out_specs=out_specs, check_vma=False)
```

```python
import math

import jax
import jax.numpy as jnp
import numpy as np
from jax import lax
from jax.experimental import pallas as pl
from jax.experimental.pallas import tpu as pltpu
from jax.sharding import PartitionSpec as P

MX = 16
MY = 16
MZ = 16
ROWS = 8
CORE_SWAP = [(0, 1), (1, 0), (2, 3), (3, 2)]
CHIP_SWAP = [(0, 2), (2, 0), (1, 3), (3, 1)]
VMEM_LIMIT = 24 * 1024 * 1024

f32 = jnp.float32
bf16 = jnp.bfloat16
exact = lax.Precision.HIGH


def waves(freqs, points, length):
    angle = 2.0 * math.pi / length * np.mod(np.outer(freqs, points), length)
    return np.cos(angle), np.sin(angle)


def complex_table(freqs, points, length):
    cosine, sine = waves(freqs, points, length)
    table = np.empty((len(freqs), 2, len(points), 2))
    table[:, 0, :, 0] = cosine
    table[:, 0, :, 1] = sine
    table[:, 1, :, 0] = -sine
    table[:, 1, :, 1] = cosine
    return table.astype(np.float32)


def real_table(freqs, points, length):
    cosine, sine = waves(freqs, points, length)
    return np.stack([cosine, -sine], 1).astype(np.float32)


def halves(table):
    table = np.asarray(table, np.float32)
    high = table.astype(bf16)
    low = (table - high.astype(np.float32)).astype(bf16)
    return jnp.asarray(high), jnp.asarray(low)


def high_low(table):
    table = np.asarray(table, np.float32)
    high = table.astype(bf16)
    return high, (table - high.astype(np.float32)).astype(bf16)


def z_tables(z_cells):
    wave = real_table(np.arange(MZ), np.arange(z_cells), z_cells).reshape(2 * MZ, z_cells)
    wave = np.einsum("kz,uv->ukvz", wave, np.eye(2, dtype=np.float32))
    high, low = high_low(wave.reshape(4 * MZ, 2 * z_cells))
    inverse = np.concatenate([high.T, low.T, high.T, low.T], axis=1)
    return jnp.asarray(np.concatenate([high, low, inverse], axis=0))


def y_tables(y_total, y_rows):
    freqs = np.concatenate([np.arange(MY), y_total - MY + np.arange(MY)])
    wave = complex_table(freqs, np.arange(y_total), y_total)
    wave = wave.reshape(2 * MY, 2, y_total // y_rows, y_rows, 2)
    table = np.einsum("jsfyr,qp->fjsqypr", wave, np.eye(4, dtype=np.float32))
    high, low = high_low(table.reshape(y_total // y_rows, 16 * MY, 8 * y_rows))
    turned = [np.swapaxes(part, 1, 2) for part in (high, low)]
    return jnp.asarray(np.concatenate([high, low] + turned, axis=1))


def product(form, left, right):
    return jnp.einsum(form, left, right, precision=exact)


def matmul(left, right):
    return jnp.dot(left, right, preferred_element_type=f32)


def matmul_t(left, right):
    return lax.dot_general(left, right, (((1,), (1,)), ((), ())), preferred_element_type=f32)


def split(value):
    high = value.astype(bf16)
    return high, (value - high.astype(f32)).astype(bf16)


def side(left, right):
    return jnp.concatenate([left, right], axis=1)


def gelu_slope(value):
    normal_cdf = 0.5 * (1.0 + lax.erf(value * (1.0 / math.sqrt(2.0))))
    return normal_cdf + value * jnp.exp(-0.5 * value * value) * (1.0 / math.sqrt(2.0 * math.pi))


def both_planes(ref, pair):
    start = 2 * pair
    shape = (2 * ref.shape[2], ref.shape[3])
    return side(ref[0, start:start + 2].reshape(shape), ref[1, start:start + 2].reshape(shape))


def put_planes(ref, pair, value):
    start = 2 * pair
    channels = ref.shape[3]
    shape = (2, ref.shape[2], channels)
    ref[0, start:start + 2] = value[:, :channels].reshape(shape)
    ref[1, start:start + 2] = value[:, channels:].reshape(shape)


def diagonal(square):
    zero = jnp.zeros_like(square)
    return jnp.concatenate([side(square, zero), side(zero, square)], axis=0)


def folded(table, value):
    result = matmul(table, value)
    count = result.shape[0] // 2
    return result[:count] + result[count:]


def first_row(half, owner):
    return pl.multiple_of(half * 16 + owner * 8, 8)


def y_forward(owner, lifted, y_table, target):
    channels = target.shape[-1]
    count = 16 * MY
    for half in range(2):
        block = lifted[:, pl.ds(first_row(half, owner), 8), :]
        high, low = split(block.reshape(block.shape[0] * 8, block.shape[2]))
        planes = folded(y_table[:2 * count], high) + matmul(y_table[:count], low)
        planes = planes.reshape(2 * MY, 8, 2 * channels)
        target[:, half, 0:8, :] = planes[:, :, :channels]
        target[:, half, 8:16, :] = planes[:, :, channels:]


def y_inverse(source, half, y_table):
    channels = source.shape[-1]
    planes = source[:, half].astype(f32)
    first = planes[:, 0:8, :].reshape(16 * MY, channels)
    second = planes[:, 8:16, :].reshape(16 * MY, channels)
    result = folded(y_table[32 * MY:], side(first, second).astype(bf16))
    return result.reshape(result.shape[0] // 8, 8, 2 * channels)


def keep_kernel(place, lifted, y_table, keep):
    y_forward(place[0], lifted, y_table, keep)


def keep_slopes_kernel(place, lifted, y_table, slopes, keep, slope_half, sems):
    copies = row_copies(slopes, slope_half, sems)
    for copy in copies:
        copy.start()
    y_forward(place[0], lifted, y_table, keep)
    for copy in copies:
        copy.wait()


def own_kernel(own, y_table, own_rows):
    for half in range(2):
        own_rows[half] = y_inverse(own, half, y_table)


def join_rows(core, own_rows, other, y_table, rows):
    for half in range(2):
        rows[:, pl.ds(first_row(half, core), 8), :] = own_rows[half]
        rows[:, pl.ds(first_row(half, 1 - core), 8), :] = y_inverse(other, half, y_table)


def z_inverse(pair, rows, z_table):
    value = rows[2 * pair:2 * pair + 2]
    high, low = split(value.reshape(4 * MZ, value.shape[2]))
    return matmul(z_table[8 * MZ:], jnp.concatenate([high, high, low, low], axis=0))


def put_lifted(lifted, pair, value):
    lifted[2 * pair:2 * pair + 2] = value.reshape(2, 2 * MZ, value.shape[1])


def row_copies(source, target, sems):
    copies = []
    count = source.shape[1] // sems.shape[0]
    for index in range(sems.shape[0]):
        span = slice(index * count, (index + 1) * count)
        copies.append(
            pltpu.make_async_copy(source.at[:, span], target.at[:, span], sems.at[index])
        )
    return copies


def put_rows(cells, target, sems, index):
    span = slice(index * ROWS, (index + 1) * ROWS)
    copy = pltpu.make_async_copy(cells.at[:, span], target.at[:, span], sems.at[index])
    copy.start()
    return copy


def lift_kernel(
    place, field, z_tables, y_tables, send, lifted, z_table, y_table, cells, sems, table_sems
):
    tables = [
        pltpu.make_async_copy(z_tables, z_table, table_sems.at[0]),
        pltpu.make_async_copy(y_tables.at[place[1]], y_table, table_sems.at[1]),
    ]
    copies = row_copies(field, cells, sems)
    for copy in (tables[0], *copies, tables[1]):
        copy.start()
    tables[0].wait()
    for pair in range(cells.shape[1] // 2):
        if pair % (ROWS // 2) == 0:
            copies[2 * pair // ROWS].wait()
        put_lifted(lifted, pair, folded(z_table[:8 * MZ], both_planes(cells, pair)))
    tables[1].wait()
    y_forward(1 - place[0], lifted, y_table, send)


def linear_rows(ref, pair, square, product_of):
    shape = (ROWS * ref.shape[2], ref.shape[3])
    span = slice(2 * pair, 2 * pair + ROWS)
    value = side(ref[0, span].reshape(shape), ref[1, span].reshape(shape))
    return product_of(value, square)


def slope_kernel(
    place, own_rows, other, field, cotangent, pointwise, bias, z_table, y_table,
    slope_half, send, lifted, rows,
):
    join_rows(place[0], own_rows, other, y_table, rows)
    square = diagonal(pointwise[...])
    shift = side(bias[...], bias[...])
    count = 2 * field.shape[2]
    for pair in range(field.shape[1] // 2):
        if pair % (ROWS // 2) == 0:
            linear = linear_rows(field, pair, square, matmul)
        start = pair % (ROWS // 2) * count
        pre = z_inverse(pair, rows, z_table) + linear[start:start + count] + shift
        slope = both_planes(cotangent, pair).astype(f32) * gelu_slope(pre)
        high, low = split(slope)
        put_planes(slope_half, pair, high)
        put_lifted(
            lifted, pair, folded(z_table[:8 * MZ], high) + matmul(z_table[:4 * MZ], low)
        )
    y_forward(1 - place[0], lifted, y_table, send)


def field_kernel(
    place, own_rows, other, slope_half, pointwise, z_table, y_table, result, rows, cells, sems
):
    copies = []
    join_rows(place[0], own_rows, other, y_table, rows)
    square = diagonal(pointwise[...])
    count = 2 * slope_half.shape[2]
    for pair in range(rows.shape[0] // 2):
        if pair % (ROWS // 2) == 0:
            linear = linear_rows(slope_half, pair, square, matmul_t)
        start = pair % (ROWS // 2) * count
        spatial = z_inverse(pair, rows, z_table)
        put_planes(cells, pair, (spatial + linear[start:start + count]).astype(bf16))
        if pair % (ROWS // 2) == ROWS // 2 - 1:
            copies.append(put_rows(cells, result, sems, 2 * pair // ROWS))
    for copy in copies:
        copy.wait()


def stage_kernel(source, target, sems):
    copies = row_copies(source, target, sems)
    for copy in copies:
        copy.start()
    for copy in copies:
        copy.wait()


def stacked_rows(values):
    parts = [split(value) for value in values]
    rows = [part[0].astype(f32) for part in parts] + [part[1].astype(f32) for part in parts]
    return jnp.concatenate(rows, axis=0)


def only(rows, pair):
    index = lax.broadcasted_iota(jnp.int32, rows.shape, 0)
    return jnp.where(index % 8 == pair, rows, 0.0).astype(bf16)


def side_weights(core, own, other, index, pair):
    block = other.at[index] if pair // 4 else own.at[index, core]
    return side(block[pair % 4, 0], block[pair % 4, 1])


def mix_kernel(place, modes, own, other, mixed):
    channels = modes.shape[-1]
    for index in range(modes.shape[0]):
        rows = stacked_rows([modes[index, 0], modes[index, 1]])
        total = jnp.zeros((32, 2 * channels), f32)
        for pair in range(8):
            weight = side_weights(place[0], own, other, index, pair)
            total = total + matmul(only(rows, pair), weight)
        real = total[0:8] + total[16:24]
        imag = total[8:16] + total[24:32]
        mixed[index, 0] = real[:, :channels] - imag[:, channels:]
        mixed[index, 1] = real[:, channels:] + imag[:, :channels]


def adjoint_kernel(place, grads, own, other, back):
    channels = grads.shape[-1]
    for index in range(grads.shape[0]):
        real, imag = grads[index, 0], grads[index, 1]
        rows = stacked_rows([side(real, imag), side(imag, -real)])
        total = jnp.zeros((32, channels), f32)
        for pair in range(8):
            weight = side_weights(place[0], own, other, index, pair)
            total = total + matmul_t(only(rows, pair), weight)
        back[index, 0] = total[0:8] + total[16:24]
        back[index, 1] = total[8:16] + total[24:32]


def outer_kernel(modes, grads, result):
    channels = modes.shape[-1]
    real, imag = grads[0, 0], grads[0, 1]
    left = stacked_rows([modes[0, 0], modes[0, 1]])
    right = stacked_rows([side(real, imag), side(imag, -real)])
    fill = channels - 48
    left = jnp.concatenate([left[:16], left[:16], left[16:], jnp.zeros((fill, channels), f32)], axis=0)
    right = jnp.concatenate([right, right[:16], jnp.zeros((fill, 2 * channels), f32)], axis=0)
    left = left.T
    right = right.astype(bf16)
    index = lax.broadcasted_iota(jnp.int32, left.shape, 1)
    for pair in range(8):
        value = matmul(jnp.where(index % 8 == pair, left, 0.0).astype(bf16), right)
        result[0, pair, 0] = value[:, :channels]
        result[0, pair, 1] = value[:, channels:]


def device_call(kernel, operands, spaces, outs, out_spaces, scratch, flops):
    operands = [
        pltpu.with_memory_space_constraint(operand, space) if space is pltpu.HBM else operand
        for operand, space in zip(operands, spaces)
    ]
    return pl.pallas_call(
        kernel,
        in_specs=[pl.BlockSpec(memory_space=space) for space in spaces],
        out_specs=[pl.BlockSpec(memory_space=space) for space in out_spaces],
        out_shape=outs,
        scratch_shapes=scratch,
        compiler_params=pltpu.CompilerParams(vmem_limit_bytes=VMEM_LIMIT),
        cost_estimate=pl.CostEstimate(flops=flops, bytes_accessed=10**6, transcendentals=0),
    )(*operands)


def modes_call(kernel, operands, out):
    def spec(array):
        rest = (0,) * (len(array.shape) - 1)
        return pl.BlockSpec((1,) + array.shape[1:], lambda step: (step,) + rest)

    return pl.pallas_call(
        kernel,
        grid=(out.shape[0],),
        in_specs=[spec(array) for array in operands],
        out_specs=spec(out),
        out_shape=out,
        compiler_params=pltpu.CompilerParams(vmem_limit_bytes=VMEM_LIMIT),
        cost_estimate=pl.CostEstimate(flops=10**9, bytes_accessed=4 * 10**6, transcendentals=0),
    )(*operands)


def own_first(pair, first):
    return jnp.where(first, pair[0], pair[1]), jnp.where(first, pair[1], pair[0])


def in_order(own, other, first):
    return jnp.where(first, own, other), jnp.where(first, other, own)


def body(fields, cotangent, spectral, pointwise, lift_bias):
    x_rows, y_rows, z_cells, channels = fields.shape
    slabs = lax.axis_size("slab")
    x_total = x_rows * slabs
    y_total = y_rows * lax.axis_size("fsdp")
    scale = 1.0 / float(x_total * y_total * z_cells)
    slab = lax.axis_index("slab")
    shard = lax.axis_index("fsdp")
    core_first = shard % 2 == 0
    chip_first = shard // 2 == 0
    place = jnp.stack([shard % 2, shard]).astype(jnp.int32)

    table_x = complex_table(np.arange(MX), np.arange(x_total), x_total)
    table_x = jnp.asarray(table_x.reshape(MX, 2, slabs, x_rows, 2))
    z_all = z_tables(z_cells)
    y_all = y_tables(y_total, y_rows)
    z_freq = (slab % 2) * 8 + (shard % 2) * 4 + jnp.arange(8, dtype=jnp.int32) % 4
    weight = jnp.where(z_freq == 0, scale, 2.0 * scale).astype(f32)
    own_weights = spectral.reshape(MX // 4, 2, 4, 2, channels, channels)
    send = lax.dynamic_index_in_dim(own_weights, 1 - shard % 2, 1, keepdims=False)
    other_weights = lax.ppermute(send, "fsdp", CORE_SWAP)

    message = jax.ShapeDtypeStruct((2 * MY, 2, 8 * x_rows, channels), f32)
    lifted_form = pltpu.VMEM((y_rows, 2 * MZ, 2 * channels), f32)
    own_form = pltpu.VMEM((2, y_rows, 8, 2 * channels), f32)

    def along(value):
        return value * weight[None, None, :, None]

    def to_modes(send, keep):
        planes = keep + lax.ppermute(send, "fsdp", CORE_SWAP)
        planes = planes.astype(bf16).reshape(slabs, x_rows * 8, channels)
        whole_x = lax.all_to_all(planes, "slab", split_axis=0, concat_axis=0, tiled=True)
        whole_x = whole_x.reshape(slabs, x_rows, 2, 4, channels).astype(f32)
        modes = product("xarqc,msxar->msqc", whole_x, table_x)
        keep, send = own_first(modes.reshape(2, MX // 2, 2, 4, channels), chip_first)
        modes = keep + lax.ppermute(send, "fsdp", CHIP_SWAP)
        return jnp.concatenate(own_first(modes.reshape(2, MX // 4, 2, 4, channels), core_first), 2)

    def regroup(modes):
        other = lax.ppermute(modes[..., 4:, :], "fsdp", CORE_SWAP)
        return jnp.concatenate(in_order(modes[..., :4, :], other, core_first), -2)

    def to_planes(modes, *beside):
        modes = jnp.concatenate(in_order(modes[:, :, :4], modes[:, :, 4:], core_first), 0)
        other = lax.ppermute(modes, "fsdp", CHIP_SWAP)
        modes = jnp.concatenate(in_order(modes, other, chip_first), 0)
        planes = product("msqc,msxar->xarqc", modes, table_x)
        planes = planes.astype(bf16).reshape(slabs, x_rows * 8, channels)
        planes = lax.all_to_all(planes, "slab", split_axis=0, concat_axis=0, tiled=True)
        planes, *beside = lax.optimization_barrier((planes, *beside))
        other = lax.ppermute(planes, "fsdp", CORE_SWAP)
        planes = planes.reshape(message.shape)
        own_rows, = device_call(
            own_kernel, (planes, y_table), (vmem, vmem), (own_form,), (vmem,), [], 10**9
        )
        return own_rows, other.reshape(message.shape), *beside

    smem, vmem, hbm = pltpu.SMEM, pltpu.VMEM, pltpu.HBM
    cells = pltpu.VMEM(fields.shape, bf16)
    sems = pltpu.SemaphoreType.DMA((y_rows // ROWS,))
    forms = (
        jax.ShapeDtypeStruct(z_all.shape, bf16), jax.ShapeDtypeStruct(y_all.shape[1:], bf16)
    )
    send, lifted, z_table, y_table = device_call(
        lift_kernel, (place, fields, z_all, y_all), (smem, hbm, hbm, hbm),
        (message, lifted_form) + forms, (vmem,) * 4,
        [cells, sems, pltpu.SemaphoreType.DMA((2,))], 10**9,
    )
    keep, = device_call(
        keep_kernel, (place, lifted, y_table), (smem, vmem, vmem), (message,), (vmem,), [], 10**9
    )
    modes = to_modes(send, keep)
    out = jax.ShapeDtypeStruct(modes.shape, f32)
    mixed, = device_call(
        mix_kernel, (place, modes, own_weights, other_weights), (smem,) + (vmem,) * 3,
        (out,), (vmem,), [], 10**9,
    )
    mixed = along(mixed)
    own_rows, other = to_planes(mixed)
    bias = lift_bias.reshape(1, channels)
    slopes, send, lifted = device_call(
        slope_kernel,
        (place, own_rows, other, fields, cotangent, pointwise, bias, z_table, y_table),
        (smem,) + (vmem,) * 8,
        (vmem(fields.shape, bf16), message, lifted_form), (vmem,) * 3,
        [lifted_form], 4 * 10**9,
    )
    keep, slope_half = device_call(
        keep_slopes_kernel, (place, lifted, y_table, slopes), (smem, vmem, vmem, vmem),
        (message, jax.ShapeDtypeStruct(fields.shape, bf16)), (vmem, hbm), [sems], 10**9,
    )
    grads = along(to_modes(send, keep))
    back, = device_call(
        adjoint_kernel, (place, grads, own_weights, other_weights), (smem,) + (vmem,) * 3,
        (out,), (vmem,), [], 10**9,
    )
    pair = regroup(jnp.stack([modes, grads]))
    weight_grads = modes_call(
        outer_kernel, (pair[0], pair[1]), jax.ShapeDtypeStruct(spectral.shape, f32)
    )
    back, slope_half = lax.optimization_barrier((back, slope_half))
    slopes, = device_call(
        stage_kernel, (slope_half,), (hbm,), (vmem(fields.shape, bf16),), (vmem,), [sems], 10**9
    )
    own_rows, other, weight_grads, slopes = to_planes(back, weight_grads, slopes)
    field_grads, = device_call(
        field_kernel, (place, own_rows, other, slopes, pointwise, z_table, y_table),
        (smem,) + (vmem,) * 6, (jax.ShapeDtypeStruct(fields.shape, bf16),), (hbm,),
        [lifted_form, cells, sems], 2 * 10**9,
    )
    return (field_grads, weight_grads)


def solution(mesh):
    in_specs = (
        P("slab", "fsdp", None, None),
        P("slab", "fsdp", None, None),
        P("fsdp", "slab", None, None, None),
        P(),
        P(),
    )
    out_specs = (P("slab", "fsdp", None, None), P("fsdp", "slab", None, None, None))
    return jax.shard_map(body, mesh=mesh, in_specs=in_specs, out_specs=out_specs, check_vma=False)
```

```python
import math

import jax
import jax.numpy as jnp
import numpy as np
from jax import lax
from jax.experimental import pallas as pl
from jax.experimental.pallas import tpu as pltpu
from jax.sharding import PartitionSpec as P

MX = 16
MY = 16
MZ = 16
ROWS = 8
CORE_SWAP = [(0, 1), (1, 0), (2, 3), (3, 2)]
CHIP_SWAP = [(0, 2), (2, 0), (1, 3), (3, 1)]
VMEM_LIMIT = 24 * 1024 * 1024

f32 = jnp.float32
bf16 = jnp.bfloat16
exact = lax.Precision.HIGH


def waves(freqs, points, length):
    angle = 2.0 * math.pi / length * np.mod(np.outer(freqs, points), length)
    return np.cos(angle), np.sin(angle)


def complex_table(freqs, points, length):
    cosine, sine = waves(freqs, points, length)
    table = np.empty((len(freqs), 2, len(points), 2))
    table[:, 0, :, 0] = cosine
    table[:, 0, :, 1] = sine
    table[:, 1, :, 0] = -sine
    table[:, 1, :, 1] = cosine
    return table.astype(np.float32)


def real_table(freqs, points, length):
    cosine, sine = waves(freqs, points, length)
    return np.stack([cosine, -sine], 1).astype(np.float32)


def halves(table):
    table = np.asarray(table, np.float32)
    high = table.astype(bf16)
    low = (table - high.astype(np.float32)).astype(bf16)
    return jnp.asarray(high), jnp.asarray(low)


def high_low(table):
    table = np.asarray(table, np.float32)
    high = table.astype(bf16)
    return high, (table - high.astype(np.float32)).astype(bf16)


def z_tables(z_cells):
    wave = real_table(np.arange(MZ), np.arange(z_cells), z_cells).reshape(2 * MZ, z_cells)
    wave = np.einsum("kz,uv->ukvz", wave, np.eye(2, dtype=np.float32))
    high, low = high_low(wave.reshape(4 * MZ, 2 * z_cells))
    inverse = np.concatenate([high.T, low.T, high.T, low.T], axis=1)
    return jnp.asarray(np.concatenate([high, low, inverse], axis=0))


def y_tables(y_total, y_rows):
    freqs = np.concatenate([np.arange(MY), y_total - MY + np.arange(MY)])
    wave = complex_table(freqs, np.arange(y_total), y_total)
    wave = wave.reshape(2 * MY, 2, y_total // y_rows, y_rows, 2)
    table = np.einsum("jsfyr,qp->fjsqypr", wave, np.eye(4, dtype=np.float32))
    high, low = high_low(table.reshape(y_total // y_rows, 16 * MY, 8 * y_rows))
    turned = [np.swapaxes(part, 1, 2) for part in (high, low)]
    return jnp.asarray(np.concatenate([high, low] + turned, axis=1))


def product(form, left, right):
    return jnp.einsum(form, left, right, precision=exact)


def matmul(left, right):
    return jnp.dot(left, right, preferred_element_type=f32)


def matmul_t(left, right):
    return lax.dot_general(left, right, (((1,), (1,)), ((), ())), preferred_element_type=f32)


def split(value):
    high = value.astype(bf16)
    return high, (value - high.astype(f32)).astype(bf16)


def side(left, right):
    return jnp.concatenate([left, right], axis=1)


def gelu_slope(value):
    normal_cdf = 0.5 * (1.0 + lax.erf(value * (1.0 / math.sqrt(2.0))))
    return normal_cdf + value * jnp.exp(-0.5 * value * value) * (1.0 / math.sqrt(2.0 * math.pi))


def both_planes(ref, pair):
    start = 2 * pair
    shape = (2 * ref.shape[2], ref.shape[3])
    return side(ref[0, start:start + 2].reshape(shape), ref[1, start:start + 2].reshape(shape))


def put_planes(ref, pair, value):
    start = 2 * pair
    channels = ref.shape[3]
    shape = (2, ref.shape[2], channels)
    ref[0, start:start + 2] = value[:, :channels].reshape(shape)
    ref[1, start:start + 2] = value[:, channels:].reshape(shape)


def diagonal(square):
    zero = jnp.zeros_like(square)
    return jnp.concatenate([side(square, zero), side(zero, square)], axis=0)


def folded(table, value):
    result = matmul(table, value)
    count = result.shape[0] // 2
    return result[:count] + result[count:]


def first_row(half, owner):
    return pl.multiple_of(half * 16 + owner * 8, 8)


def y_forward(owner, lifted, y_table, target):
    channels = target.shape[-1]
    count = 16 * MY
    for half in range(2):
        block = lifted[:, pl.ds(first_row(half, owner), 8), :]
        high, low = split(block.reshape(block.shape[0] * 8, block.shape[2]))
        planes = folded(y_table[:2 * count], high) + matmul(y_table[:count], low)
        planes = planes.reshape(2 * MY, 8, 2 * channels)
        planes = jnp.concatenate([planes[:, :, :channels], planes[:, :, channels:]], axis=1)
        target[:, half] = planes.astype(target.dtype)


def y_inverse(source, half, y_table):
    channels = source.shape[-1]
    planes = source[:, half].astype(f32)
    first = planes[:, 0:8, :].reshape(16 * MY, channels)
    second = planes[:, 8:16, :].reshape(16 * MY, channels)
    result = folded(y_table[32 * MY:], side(first, second).astype(bf16))
    return result.reshape(result.shape[0] // 8, 8, 2 * channels)


def keep_kernel(place, lifted, y_table, keep):
    y_forward(place[0], lifted, y_table, keep)


def keep_slopes_kernel(place, lifted, y_table, slopes, keep, slope_half, sems):
    copies = row_copies(slopes, slope_half, sems)
    for copy in copies:
        copy.start()
    y_forward(place[0], lifted, y_table, keep)
    for copy in copies:
        copy.wait()


def own_kernel(own, y_table, own_rows):
    for half in range(2):
        own_rows[half] = y_inverse(own, half, y_table)


def join_rows(core, own_rows, other, y_table, rows):
    for half in range(2):
        rows[:, pl.ds(first_row(half, core), 8), :] = own_rows[half]
        rows[:, pl.ds(first_row(half, 1 - core), 8), :] = y_inverse(other, half, y_table)


def z_inverse(pair, rows, z_table):
    value = rows[2 * pair:2 * pair + 2]
    high, low = split(value.reshape(4 * MZ, value.shape[2]))
    return matmul(z_table[8 * MZ:], jnp.concatenate([high, high, low, low], axis=0))


def put_lifted(lifted, pair, value):
    lifted[2 * pair:2 * pair + 2] = value.reshape(2, 2 * MZ, value.shape[1])


def row_copies(source, target, sems):
    copies = []
    count = source.shape[1] // sems.shape[0]
    for index in range(sems.shape[0]):
        span = slice(index * count, (index + 1) * count)
        copies.append(
            pltpu.make_async_copy(source.at[:, span], target.at[:, span], sems.at[index])
        )
    return copies


def put_rows(cells, target, sems, index):
    span = slice(index * ROWS, (index + 1) * ROWS)
    copy = pltpu.make_async_copy(cells.at[:, span], target.at[:, span], sems.at[index])
    copy.start()
    return copy


def lift_kernel(
    place, field, z_tables, y_tables, send, lifted, z_table, y_table, cells, sems, table_sems
):
    tables = [
        pltpu.make_async_copy(z_tables, z_table, table_sems.at[0]),
        pltpu.make_async_copy(y_tables.at[place[1]], y_table, table_sems.at[1]),
    ]
    copies = row_copies(field, cells, sems)
    for copy in (tables[0], *copies, tables[1]):
        copy.start()
    tables[0].wait()
    for pair in range(cells.shape[1] // 2):
        if pair % (ROWS // 2) == 0:
            copies[2 * pair // ROWS].wait()
        put_lifted(lifted, pair, folded(z_table[:8 * MZ], both_planes(cells, pair)))
    tables[1].wait()
    y_forward(1 - place[0], lifted, y_table, send)


def linear_rows(ref, pair, square, product_of):
    shape = (ROWS * ref.shape[2], ref.shape[3])
    span = slice(2 * pair, 2 * pair + ROWS)
    value = side(ref[0, span].reshape(shape), ref[1, span].reshape(shape))
    return product_of(value, square)


def slope_kernel(
    place, own_rows, other, field, cotangent, pointwise, bias, z_table, y_table,
    slope_half, send, lifted, rows,
):
    join_rows(place[0], own_rows, other, y_table, rows)
    square = diagonal(pointwise[...])
    shift = side(bias[...], bias[...])
    count = 2 * field.shape[2]
    for pair in range(field.shape[1] // 2):
        if pair % (ROWS // 2) == 0:
            linear = linear_rows(field, pair, square, matmul)
        start = pair % (ROWS // 2) * count
        pre = z_inverse(pair, rows, z_table) + linear[start:start + count] + shift
        slope = both_planes(cotangent, pair).astype(f32) * gelu_slope(pre)
        high, low = split(slope)
        put_planes(slope_half, pair, high)
        put_lifted(
            lifted, pair, folded(z_table[:8 * MZ], high) + matmul(z_table[:4 * MZ], low)
        )
    y_forward(1 - place[0], lifted, y_table, send)


def field_kernel(
    place, own_rows, other, slope_half, pointwise, z_table, y_table, result, rows, cells, sems
):
    copies = []
    join_rows(place[0], own_rows, other, y_table, rows)
    square = diagonal(pointwise[...])
    count = 2 * slope_half.shape[2]
    for pair in range(rows.shape[0] // 2):
        if pair % (ROWS // 2) == 0:
            linear = linear_rows(slope_half, pair, square, matmul_t)
        start = pair % (ROWS // 2) * count
        spatial = z_inverse(pair, rows, z_table)
        put_planes(cells, pair, (spatial + linear[start:start + count]).astype(bf16))
        if pair % (ROWS // 2) == ROWS // 2 - 1:
            copies.append(put_rows(cells, result, sems, 2 * pair // ROWS))
    for copy in copies:
        copy.wait()


def stage_kernel(source, target, sems):
    copies = row_copies(source, target, sems)
    for copy in copies:
        copy.start()
    for copy in copies:
        copy.wait()


def stacked_rows(values):
    parts = [split(value) for value in values]
    rows = [part[0].astype(f32) for part in parts] + [part[1].astype(f32) for part in parts]
    return jnp.concatenate(rows, axis=0)


def only(rows, pair):
    index = lax.broadcasted_iota(jnp.int32, rows.shape, 0)
    return jnp.where(index % 8 == pair, rows, 0.0).astype(bf16)


def side_weights(core, own, other, index, pair):
    block = other.at[index] if pair // 4 else own.at[index, core]
    return side(block[pair % 4, 0], block[pair % 4, 1])


def mix_kernel(place, modes, own, other, mixed):
    channels = modes.shape[-1]
    for index in range(modes.shape[0]):
        rows = stacked_rows([modes[index, 0], modes[index, 1]])
        total = jnp.zeros((32, 2 * channels), f32)
        for pair in range(8):
            weight = side_weights(place[0], own, other, index, pair)
            total = total + matmul(only(rows, pair), weight)
        real = total[0:8] + total[16:24]
        imag = total[8:16] + total[24:32]
        mixed[index, 0] = real[:, :channels] - imag[:, channels:]
        mixed[index, 1] = real[:, channels:] + imag[:, :channels]


def adjoint_kernel(place, grads, own, other, back):
    channels = grads.shape[-1]
    for index in range(grads.shape[0]):
        real, imag = grads[index, 0], grads[index, 1]
        rows = stacked_rows([side(real, imag), side(imag, -real)])
        total = jnp.zeros((32, channels), f32)
        for pair in range(8):
            weight = side_weights(place[0], own, other, index, pair)
            total = total + matmul_t(only(rows, pair), weight)
        back[index, 0] = total[0:8] + total[16:24]
        back[index, 1] = total[8:16] + total[24:32]


def outer_kernel(modes, grads, result):
    channels = modes.shape[-1]
    real, imag = grads[0, 0], grads[0, 1]
    left = stacked_rows([modes[0, 0], modes[0, 1]])
    right = stacked_rows([side(real, imag), side(imag, -real)])
    fill = channels - 48
    left = jnp.concatenate([left[:16], left[:16], left[16:], jnp.zeros((fill, channels), f32)], axis=0)
    right = jnp.concatenate([right, right[:16], jnp.zeros((fill, 2 * channels), f32)], axis=0)
    left = left.T
    right = right.astype(bf16)
    index = lax.broadcasted_iota(jnp.int32, left.shape, 1)
    for pair in range(8):
        value = matmul(jnp.where(index % 8 == pair, left, 0.0).astype(bf16), right)
        result[0, pair, 0] = value[:, :channels]
        result[0, pair, 1] = value[:, channels:]


def device_call(kernel, operands, spaces, outs, out_spaces, scratch, flops):
    operands = [
        pltpu.with_memory_space_constraint(operand, space) if space is pltpu.HBM else operand
        for operand, space in zip(operands, spaces)
    ]
    return pl.pallas_call(
        kernel,
        in_specs=[pl.BlockSpec(memory_space=space) for space in spaces],
        out_specs=[pl.BlockSpec(memory_space=space) for space in out_spaces],
        out_shape=outs,
        scratch_shapes=scratch,
        compiler_params=pltpu.CompilerParams(vmem_limit_bytes=VMEM_LIMIT),
        cost_estimate=pl.CostEstimate(flops=flops, bytes_accessed=10**6, transcendentals=0),
    )(*operands)


def modes_call(kernel, operands, out):
    def spec(array):
        rest = (0,) * (len(array.shape) - 1)
        return pl.BlockSpec((1,) + array.shape[1:], lambda step: (step,) + rest)

    return pl.pallas_call(
        kernel,
        grid=(out.shape[0],),
        in_specs=[spec(array) for array in operands],
        out_specs=spec(out),
        out_shape=out,
        compiler_params=pltpu.CompilerParams(vmem_limit_bytes=VMEM_LIMIT),
        cost_estimate=pl.CostEstimate(flops=10**9, bytes_accessed=4 * 10**6, transcendentals=0),
    )(*operands)


def own_first(pair, first):
    return jnp.where(first, pair[0], pair[1]), jnp.where(first, pair[1], pair[0])


def in_order(own, other, first):
    return jnp.where(first, own, other), jnp.where(first, other, own)


def body(fields, cotangent, spectral, pointwise, lift_bias):
    x_rows, y_rows, z_cells, channels = fields.shape
    slabs = lax.axis_size("slab")
    x_total = x_rows * slabs
    y_total = y_rows * lax.axis_size("fsdp")
    scale = 1.0 / float(x_total * y_total * z_cells)
    slab = lax.axis_index("slab")
    shard = lax.axis_index("fsdp")
    core_first = shard % 2 == 0
    chip_first = shard // 2 == 0
    place = jnp.stack([shard % 2, shard]).astype(jnp.int32)

    table_x = complex_table(np.arange(MX), np.arange(x_total), x_total)
    table_x = jnp.asarray(table_x.reshape(MX, 2, slabs, x_rows, 2))
    z_all = z_tables(z_cells)
    y_all = y_tables(y_total, y_rows)
    z_freq = (slab % 2) * 8 + (shard % 2) * 4 + jnp.arange(8, dtype=jnp.int32) % 4
    weight = jnp.where(z_freq == 0, scale, 2.0 * scale).astype(f32)
    own_weights = spectral.reshape(MX // 4, 2, 4, 2, channels, channels)
    send = lax.dynamic_index_in_dim(own_weights, 1 - shard % 2, 1, keepdims=False)
    other_weights = lax.ppermute(send, "fsdp", CORE_SWAP)

    message = jax.ShapeDtypeStruct((2 * MY, 2, 8 * x_rows, channels), f32)
    sent = jax.ShapeDtypeStruct(message.shape, bf16)
    lifted_form = pltpu.VMEM((y_rows, 2 * MZ, 2 * channels), f32)
    own_form = pltpu.VMEM((2, y_rows, 8, 2 * channels), f32)

    def along(value):
        return value * weight[None, None, :, None]

    def to_modes(send, keep):
        planes = keep + lax.ppermute(send, "fsdp", CORE_SWAP).astype(f32)
        planes = planes.astype(bf16).reshape(slabs, x_rows * 8, channels)
        whole_x = lax.all_to_all(planes, "slab", split_axis=0, concat_axis=0, tiled=True)
        whole_x = whole_x.reshape(slabs, x_rows, 2, 4, channels).astype(f32)
        modes = product("xarqc,msxar->msqc", whole_x, table_x)
        keep, send = own_first(modes.reshape(2, MX // 2, 2, 4, channels), chip_first)
        modes = keep + lax.ppermute(send, "fsdp", CHIP_SWAP)
        return jnp.concatenate(own_first(modes.reshape(2, MX // 4, 2, 4, channels), core_first), 2)

    def regroup(modes):
        other = lax.ppermute(modes[..., 4:, :], "fsdp", CORE_SWAP)
        return jnp.concatenate(in_order(modes[..., :4, :], other, core_first), -2)

    def to_planes(modes, *beside):
        modes = jnp.concatenate(in_order(modes[:, :, :4], modes[:, :, 4:], core_first), 0)
        other = lax.ppermute(modes, "fsdp", CHIP_SWAP)
        modes = jnp.concatenate(in_order(modes, other, chip_first), 0)
        planes = product("msqc,msxar->xarqc", modes, table_x)
        planes = planes.astype(bf16).reshape(slabs, x_rows * 8, channels)
        planes = lax.all_to_all(planes, "slab", split_axis=0, concat_axis=0, tiled=True)
        planes, *beside = lax.optimization_barrier((planes, *beside))
        other = lax.ppermute(planes, "fsdp", CORE_SWAP)
        planes = planes.reshape(message.shape)
        own_rows, = device_call(
            own_kernel, (planes, y_table), (vmem, vmem), (own_form,), (vmem,), [], 10**9
        )
        return own_rows, other.reshape(message.shape), *beside

    smem, vmem, hbm = pltpu.SMEM, pltpu.VMEM, pltpu.HBM
    cells = pltpu.VMEM(fields.shape, bf16)
    sems = pltpu.SemaphoreType.DMA((y_rows // ROWS,))
    forms = (
        jax.ShapeDtypeStruct(z_all.shape, bf16), jax.ShapeDtypeStruct(y_all.shape[1:], bf16)
    )
    send, lifted, z_table, y_table = device_call(
        lift_kernel, (place, fields, z_all, y_all), (smem, hbm, hbm, hbm),
        (sent, lifted_form) + forms, (vmem,) * 4,
        [cells, sems, pltpu.SemaphoreType.DMA((2,))], 10**9,
    )
    keep, = device_call(
        keep_kernel, (place, lifted, y_table), (smem, vmem, vmem), (message,), (vmem,), [], 10**9
    )
    modes = to_modes(send, keep)
    out = jax.ShapeDtypeStruct(modes.shape, f32)
    mixed, = device_call(
        mix_kernel, (place, modes, own_weights, other_weights), (smem,) + (vmem,) * 3,
        (out,), (vmem,), [], 10**9,
    )
    mixed = along(mixed)
    own_rows, other = to_planes(mixed)
    bias = lift_bias.reshape(1, channels)
    slopes, send, lifted = device_call(
        slope_kernel,
        (place, own_rows, other, fields, cotangent, pointwise, bias, z_table, y_table),
        (smem,) + (vmem,) * 8,
        (vmem(fields.shape, bf16), sent, lifted_form), (vmem,) * 3,
        [lifted_form], 4 * 10**9,
    )
    keep, slope_half = device_call(
        keep_slopes_kernel, (place, lifted, y_table, slopes), (smem, vmem, vmem, vmem),
        (message, jax.ShapeDtypeStruct(fields.shape, bf16)), (vmem, hbm), [sems], 10**9,
    )
    grads = along(to_modes(send, keep))
    back, = device_call(
        adjoint_kernel, (place, grads, own_weights, other_weights), (smem,) + (vmem,) * 3,
        (out,), (vmem,), [], 10**9,
    )
    pair = regroup(jnp.stack([modes, grads]))
    weight_grads = modes_call(
        outer_kernel, (pair[0], pair[1]), jax.ShapeDtypeStruct(spectral.shape, f32)
    )
    back, slope_half = lax.optimization_barrier((back, slope_half))
    slopes, = device_call(
        stage_kernel, (slope_half,), (hbm,), (vmem(fields.shape, bf16),), (vmem,), [sems], 10**9
    )
    own_rows, other, weight_grads, slopes = to_planes(back, weight_grads, slopes)
    field_grads, = device_call(
        field_kernel, (place, own_rows, other, slopes, pointwise, z_table, y_table),
        (smem,) + (vmem,) * 6, (jax.ShapeDtypeStruct(fields.shape, bf16),), (hbm,),
        [lifted_form, cells, sems], 2 * 10**9,
    )
    return (field_grads, weight_grads)


def solution(mesh):
    in_specs = (
        P("slab", "fsdp", None, None),
        P("slab", "fsdp", None, None),
        P("fsdp", "slab", None, None, None),
        P(),
        P(),
    )
    out_specs = (P("slab", "fsdp", None, None), P("fsdp", "slab", None, None, None))
    return jax.shard_map(body, mesh=mesh, in_specs=in_specs, out_specs=out_specs, check_vma=False)
```
